32 devices in a mesh: runs: 2 (over y), gx: 16 (over z, x, core).
Axes of the slice: x: 2, y: 2, z: 4, core: 2. Of those that a mesh axis runs over, the one named last changes fastest.
Arguments:
- velocity: float32 [6, 64, 128, 128], P('runs', 'gx'), parts along dimension 0, may hold values from -4 to 4
- inflow: float32 [6, 128, 128], P('runs', 'gx'), parts along dimension 0, may hold values from -4 to 4
- blade_motion: float32 [6, 3072], P('runs', 'gx'), parts along dimension 0, may hold values from -6 to 6
- blade_axis: float32 [6, 3072], P('runs', 'gx'), parts along dimension 0, may hold values from -1 to 1
- blade_chord: float32 [6144], P(('runs', 'gx')), parts along dimension 0, may hold values from 0.3 to 1.5
- host_cell: int32 [6144], P(('runs', 'gx')), parts along dimension 0, may hold values from -1 to 49150, as said below
- host_frac: float32 [6, 3072], P('runs', 'gx'), parts along dimension 0, may hold values from 0 to 1
Outputs:
- new_velocity: float32 [6, 64, 128, 128], P('runs', 'gx'), parts along dimension 0
The draws below stay inside these ranges and needn't reach their ends.
There are 2 independent parts, one for each index of `runs`. The reference program is written for one: setup_inputs(seed, part) draws one part's arguments, and reference() takes and returns one part's arrays. A program takes and returns all parts, laid end to end along the dimension named above; each array names one. Nothing has to cross between parts.
Inputs may be any that keep to these rules, and one draw needn't show every extreme that they name: `host_cell`: each tile's slots form 16 blocks of 12, block o for blade points owned by device o; slot o * 12 + c of tile t holds owner o's blade point t * 12 + c (that point's data are unused where the slot is empty). Blade points are assigned to owners without regard to their position. A quarter of all tiles are rotor tiles; occupied slots lie only in tiles whose index differs from some rotor tile's by at most one. An occupied slot's cell has streamwise index at most 2 and vertical index at most 126 within its tile. Empty slots may stand anywhere. In every draw some owner's block is full in every tile within one of some rotor tile.
All inputs are finite; a program needn't handle non-finite values.
Results may differ from the reference program's by a relative error of at most 0.00002.
Values sent between devices are 32-bit elements; how exact they have to be, the bound alone decides.
A program may use at most 128 MiB of HBM per device.

```python
import math
import jax
import jax.numpy as jnp
from jax import lax

CX = 4
NY = 128
NZ = 128
CAP = 12
JACOBI = 3
NX = 64
P_ALL = 3072
N_GX = 16


def draw_velocity(key, part):
    values = jnp.clip(jax.random.normal(key, (3, NX, NY, NZ), jnp.float32), -4.0, 4.0)
    return values


def draw_host_cell(key, part):
    key = jax.random.fold_in(key, 5)
    key_tiles, key_owner, key_fill, key_stream, key_span, key_depth, key_pick = jax.random.split(key, 7)
    slot_count = N_GX * CAP
    order = jax.random.permutation(key_tiles, N_GX)
    row_tiles = order[:N_GX // 4]
    first_rotor = order[0]
    tile_ids = jnp.arange(N_GX, dtype=jnp.int32)
    near_tile = jnp.any(jnp.abs(tile_ids[:, None] - row_tiles[None, :]) <= 1, axis=1)
    full_owner = jax.random.randint(key_owner, (), 0, N_GX)
    owner_dev = jnp.arange(slot_count, dtype=jnp.int32) // CAP
    coin = jax.random.randint(key_fill, (N_GX, slot_count), 0, 8)
    filled = near_tile[:, None] & ((coin != 0) | (owner_dev[None, :] == full_owner))
    stream_pos = jax.random.randint(key_stream, (N_GX, slot_count), 0, CX - 1)
    span_pos = jax.random.randint(key_span, (N_GX, slot_count), 0, NY)
    depth_pos = jax.random.randint(key_depth, (N_GX, slot_count), 0, NZ - 1)
    cells = stream_pos * (NY * NZ) + span_pos * NZ + depth_pos
    pick = jax.random.randint(key_pick, (), 0, CAP)
    top_cell = (CX - 2) * NY * NZ + (NY - 1) * NZ + NZ - 2
    chosen = (jnp.arange(slot_count)[None, :] == full_owner * CAP + pick) & (tile_ids[:, None] == first_rotor)
    cells = jnp.where(chosen, top_cell, cells)
    return jnp.where(filled, cells, -1).reshape(-1).astype(jnp.int32)


def steps_of(key, extent, shards, low, high):
    gain, own = 1.0, jax.random.fold_in(key, 6)
    for position, shards_of in shards:
        heights = jnp.exp(jax.random.uniform(jax.random.fold_in(own, position), (shards_of,), jnp.float32, low / len(shards), high / len(shards)))
        gain = gain * jnp.repeat(heights, extent[position] // shards_of).reshape([-1 if axis == position else 1 for axis in range(len(extent))])
    return gain


def scatter_about(own_key, extent, deviation, limit, shards=(), kind=jnp.bfloat16):
    result = jax.random.normal(own_key, extent, jnp.float32) * deviation
    if len(shards) > 0:
        result = steps_of(own_key, extent, shards, -0.22, 0.18) * result
    return jnp.clip(result, min=-limit, max=limit).astype(kind)


def setup_inputs(seed: int = 0, part: int = 0) -> dict:
    splits = jax.random.split(jax.random.key(seed), 8)
    part_keys = jax.random.split(jax.random.fold_in(splits[7], part), 8)
    return {
        "velocity": draw_velocity(jax.random.fold_in(jax.random.fold_in(splits[7], part), 71), part),
        "inflow": scatter_about(part_keys[1], (3, NY, NZ), 1.0, 4.0, ((1, 16),), jnp.float32),
        "blade_motion": scatter_about(part_keys[2], (3, P_ALL), 1.5, 6.0, ((1, 16),), jnp.float32),
        "blade_axis": jnp.clip(jax.random.uniform(part_keys[3], (3, P_ALL), jnp.float32, -1.0, 1.0) * steps_of(part_keys[3], (3, P_ALL), ((1, 16),), -0.4, 0.0), -1.0, 1.0),
        "blade_chord": jnp.clip(jnp.exp(math.log(1.5) - 1.60943787 * jax.random.uniform(part_keys[4], (P_ALL,), jnp.float32) ** steps_of(part_keys[4], (P_ALL,), ((0, 16),), -0.2, 0.2)), 0.3, 1.5),
        "host_cell": draw_host_cell(jax.random.fold_in(jax.random.fold_in(splits[7], part), 71), part),
        "host_frac": jnp.clip(1.0 * jax.random.uniform(part_keys[6], (3, N_GX * N_GX * CAP), jnp.float32) ** steps_of(part_keys[6], (3, N_GX * N_GX * CAP), ((1, 16),), -0.2, 0.2), 0.0, 1.0),
    }


TIME_STEP = 0.2
SMAGORINSKY = 0.0289
STRAIN_FLOOR = 0.01
FORCE_SCALE = 0.2

def pad_depth(values, margin):
    spec = [(0, 0)] * (values.ndim - 1) + [(margin, margin)]
    return jnp.pad(values, spec)

def pad_stream(values):
    spec = [(1, 1)] + [(0, 0)] * (values.ndim - 1)
    return jnp.pad(values, spec)

def roll_span(values, shift_by):
    return jnp.roll(values, shift_by, axis=-2)

def tensor_of(padded):
    grad_x = 0.5 * (padded[:, 2:, :, 1:-1] - padded[:, :-2, :, 1:-1])
    middle = padded[:, 1:-1, :, 1:-1]
    grad_y = 0.5 * (roll_span(middle, -1) - roll_span(middle, 1))
    grad_z = 0.5 * (padded[:, 1:-1, :, 2:] - padded[:, 1:-1, :, :-2])
    return [[grad_x[comp], grad_y[comp], grad_z[comp]] for comp in range(3)]

def eddy_viscosity(table):
    shear_sum = jnp.zeros_like(table[0][0])
    for row_i in range(3):
        for col_j in range(3):
            pair_sum = table[row_i][col_j] + table[col_j][row_i]
            shear_sum = shear_sum + 0.5 * pair_sum * pair_sum
    return SMAGORINSKY * jnp.sqrt(shear_sum + STRAIN_FLOOR)

def tendency(interior, viscosity, table):
    centre_nu = viscosity[1:-1, :, 1:-1]
    centre_u = interior[:, 1:-1, :, 1:-1]

    def face_flux(nu_side, u_side):
        return 0.5 * (centre_nu + nu_side) * (u_side - centre_u)
    diffusion = face_flux(viscosity[2:, :, 1:-1], interior[:, 2:, :, 1:-1])
    diffusion = diffusion + face_flux(viscosity[:-2, :, 1:-1], interior[:, :-2, :, 1:-1])
    diffusion = diffusion + face_flux(roll_span(centre_nu, -1), roll_span(centre_u, -1))
    diffusion = diffusion + face_flux(roll_span(centre_nu, 1), roll_span(centre_u, 1))
    diffusion = diffusion + face_flux(viscosity[1:-1, :, 2:], interior[:, 1:-1, :, 2:])
    diffusion = diffusion + face_flux(viscosity[1:-1, :, :-2], interior[:, 1:-1, :, :-2])
    rows = []
    for comp in range(3):
        carried = centre_u[0] * table[comp][0] + centre_u[1] * table[comp][1] + centre_u[2] * table[comp][2]
        rows.append(carried)
    return diffusion - jnp.stack(rows)

def momentum(extended):
    padded = pad_depth(extended, 2)
    table = tensor_of(padded)
    viscosity = eddy_viscosity(table)
    centre_table = [[entry[1:-1, :, 1:-1] for entry in row] for row in table]
    return tendency(padded[:, 1:-1, :, 1:-1], viscosity, centre_table)

def corner_weights(cells, fractions, span_cells, depth_cells):
    plane_cells = span_cells * depth_cells
    lower_cell = jnp.maximum(cells, 0)
    stream_pos = lower_cell // plane_cells
    span_pos = lower_cell // depth_cells % span_cells
    depth_pos = lower_cell % depth_cells
    occupied = jnp.where(cells >= 0, 1.0, 0.0).astype(fractions.dtype)
    corner_list = []
    weight_list = []
    for shift_x in (0, 1):
        for shift_y in (0, 1):
            for shift_z in (0, 1):
                corner_list.append((stream_pos + shift_x) * plane_cells + (span_pos + shift_y) % span_cells * depth_cells + depth_pos + shift_z)
                weight_x = fractions[0] if shift_x == 1 else 1.0 - fractions[0]
                weight_y = fractions[1] if shift_y == 1 else 1.0 - fractions[1]
                weight_z = fractions[2] if shift_z == 1 else 1.0 - fractions[2]
                weight_list.append(occupied * weight_x * weight_y * weight_z)
    return (jnp.stack(corner_list), jnp.stack(weight_list))

def blade_force(sampled, motion, direction, chord_row):
    relative = sampled - motion
    relative_speed = jnp.sqrt(lax.optimization_barrier(jnp.sum(relative * relative, axis=0)) + STRAIN_FLOOR)
    lift_dir = jnp.stack([relative[1] * direction[2] - relative[2] * direction[1], relative[2] * direction[0] - relative[0] * direction[2], relative[0] * direction[1] - relative[1] * direction[0]])
    return FORCE_SCALE * chord_row * relative_speed * (lift_dir - relative)

def divergence(rim):
    padded = pad_depth(rim, 1)
    part_x = 0.5 * (padded[0, 2:, :, 1:-1] - padded[0, :-2, :, 1:-1])
    middle = padded[1, 1:-1, :, 1:-1]
    part_y = 0.5 * (roll_span(middle, -1) - roll_span(middle, 1))
    part_z = 0.5 * (padded[2, 1:-1, :, 2:] - padded[2, 1:-1, :, :-2])
    return part_x + part_y + part_z

def jacobi_step(potential_ext, source):
    padded = pad_depth(potential_ext, 1)
    centre = padded[1:-1, :, 1:-1]
    neighbour_sum = padded[2:, :, 1:-1] + padded[:-2, :, 1:-1]
    neighbour_sum = neighbour_sum + roll_span(centre, -1) + roll_span(centre, 1)
    neighbour_sum = neighbour_sum + padded[1:-1, :, 2:] + padded[1:-1, :, :-2]
    return (neighbour_sum - source) / 6.0

def correct(provisional, potential_ext):
    padded = pad_depth(potential_ext, 1)
    centre = padded[1:-1, :, 1:-1]
    grad_x = 0.5 * (padded[2:, :, 1:-1] - padded[:-2, :, 1:-1])
    grad_y = 0.5 * (roll_span(centre, -1) - roll_span(centre, 1))
    grad_z = 0.5 * (padded[1:-1, :, 2:] - padded[1:-1, :, :-2])
    return provisional - jnp.stack([grad_x, grad_y, grad_z])

def reference(velocity, inflow, blade_motion, blade_axis, blade_chord, host_cell, host_frac):
    planes = jnp.stack([inflow, inflow], axis=1)
    blank_planes = jnp.zeros((3, 2, NY, NZ), jnp.float32)
    extended = jnp.concatenate([planes, velocity, blank_planes], axis=1)

    def tile_tendency(tile_index):
        tile_block = lax.dynamic_slice_in_dim(extended, tile_index * CX, CX + 4, 1)
        return momentum(tile_block)
    stacked = lax.map(tile_tendency, jnp.arange(N_GX, dtype=jnp.int32))
    tendency_all = jnp.transpose(stacked, (1, 0, 2, 3, 4)).reshape(3, NX, NY, NZ)
    slot_count = N_GX * N_GX * CAP
    slot_ids = jnp.arange(slot_count, dtype=jnp.int32)
    host_tile = slot_ids // (N_GX * CAP)
    owner_dev = slot_ids // CAP % N_GX
    within = slot_ids % CAP
    blade_ids = (owner_dev * N_GX + host_tile) * CAP + within
    global_cells = jnp.where(host_cell >= 0, host_cell + host_tile * (CX * NY * NZ), -1)
    corners, weights = corner_weights(global_cells, host_frac, NY, NZ)
    flat_velocity = velocity.reshape(3, NX * NY * NZ)
    sampled = lax.optimization_barrier(jnp.sum(weights[None] * flat_velocity[:, corners], axis=1))
    forces = blade_force(sampled, blade_motion[:, blade_ids], blade_axis[:, blade_ids], blade_chord[blade_ids])
    spread = jnp.zeros((3, NX * NY * NZ), jnp.float32).at[:, corners.reshape(-1)].add((forces[:, None, :] * weights[None]).reshape(3, -1))
    provisional = velocity + TIME_STEP * (tendency_all + spread.reshape(3, NX, NY, NZ))
    rim_plane = jnp.zeros((3, 1, NY, NZ), jnp.float32)
    source = divergence(jnp.concatenate([rim_plane, provisional, rim_plane], axis=1))
    potential = -source / 6.0
    for sweep_no in range(JACOBI - 1):
        potential = jacobi_step(pad_stream(potential), source)
    return correct(provisional, pad_stream(potential))
```

```python
import functools

import jax
import jax.numpy as jnp
from jax import lax
from jax.experimental import pallas as pl
from jax.experimental.pallas import tpu as pltpu
from jax.sharding import PartitionSpec as P

TIME_STEP = 0.2
SMAGORINSKY = 0.0289
STRAIN_FLOOR = 0.01
FORCE_SCALE = 0.2

MESH = pl.DeviceIdType.MESH
PAD = 8
ROWS = 16
SLOT = 16
LANES = 128


def split(value):
    high = value.astype(jnp.bfloat16)
    return high, (value - high.astype(jnp.float32)).astype(jnp.bfloat16)


def product(left, right, contract):
    def one(a, b):
        return lax.dot_general(
            a, b, (contract, ((), ())), preferred_element_type=jnp.float32
        )

    return one(left[0], right[0]) + (one(left[0], right[1]) + one(left[1], right[0]))


def kernel(
    n,
    vel,
    inflow,
    motion,
    axis,
    chord,
    cell,
    frac,
    out,
    u,
    nu,
    prov,
    p1,
    p2,
    p3,
    part_out,
    part_in,
    rows,
    blocks,
    table,
    arrived,
    inlet,
    load_sem,
    halo_send,
    halo_recv,
    blade_send,
    blade_recv,
    in_send,
    in_recv,
    rim_send,
    rim_recv,
):
    me = lax.axis_index("gx")
    cx, ny, nz = vel.shape[1:]
    cap = cell.shape[1] // n
    body = pl.ds(PAD, ny)
    has_low, has_high = me > 0, me < n - 1
    low_ok = jnp.where(has_low, 1.0, 0.0)
    high_ok = jnp.where(has_high, 1.0, 0.0)

    barrier = pltpu.get_barrier_semaphore()

    def greet(k, carry):
        pl.semaphore_signal(
            barrier, inc=1, device_id={"gx": lax.rem(me + k, n)}, device_id_type=MESH
        )
        return carry

    lax.fori_loop(1, n, greet, 0)
    load = pltpu.make_async_copy(vel, u.at[:, 2 : 2 + cx, body], load_sem)
    load.start()

    zeros = jnp.zeros((16, rows.shape[1]), jnp.float32)
    rows[...] = zeros
    rows[0:3] = motion[...]
    rows[3:6] = axis[...]
    rows[6:7] = chord[...]
    rows[8:9] = (cell[...] + 1).astype(jnp.float32)
    rows[9:12] = frac[...]
    owners = 256 // SLOT
    wide = owners * cap
    source_lane = lax.broadcasted_iota(jnp.int32, (wide, 256), 0)
    slot_lane = lax.broadcasted_iota(jnp.int32, (wide, 256), 1)
    within = slot_lane & (SLOT - 1)
    picked = (source_lane == (slot_lane >> 4) * cap + within) & (within < cap)
    pick = jnp.where(picked, 1.0, 0.0)
    chunks = n // owners
    for q in range(chunks):
        spaced = lax.dot_general(
            rows[:, q * wide : (q + 1) * wide],
            pick,
            (((1,), (0,)), ((), ())),
            precision=lax.Precision.HIGHEST,
            preferred_element_type=jnp.float32,
        )
        table[q] = spaced[8:16]
        for h in range(256 // LANES):
            blocks[q * (256 // LANES) + h] = spaced[0:8, h * LANES : (h + 1) * LANES]

    def halo(up):
        if up:
            src, dst, to = vel.at[:, cx - 2 : cx], u.at[:, 0:2, body], me + 1
        else:
            src, dst, to = vel.at[:, 0:2], u.at[:, cx + 2 : cx + 4, body], me - 1
        return pltpu.make_async_remote_copy(
            src_ref=src,
            dst_ref=dst,
            send_sem=halo_send.at[int(up)],
            recv_sem=halo_recv.at[int(up)],
            device_id={"gx": to},
            device_id_type=MESH,
        )

    per = LANES // SLOT

    def blade(k, to, slot):
        return pltpu.make_async_remote_copy(
            src_ref=blocks.at[to // per],
            dst_ref=arrived.at[slot],
            send_sem=blade_send.at[k],
            recv_sem=blade_recv.at[k],
            device_id={"gx": to},
            device_id_type=MESH,
        )

    def feed(slot):
        return pltpu.make_async_remote_copy(
            src_ref=inflow,
            dst_ref=inlet.at[slot],
            send_sem=in_send,
            recv_sem=in_recv.at[slot],
            device_id={"gx": 0},
            device_id_type=MESH,
        )

    pl.semaphore_wait(barrier, n - 1)

    @pl.when(has_low)
    def _():
        feed(me).start()
        halo(False).start()

    @pl.when(has_high)
    def _():
        halo(True).start()

    def send_blade(k, carry):
        blade(k, lax.rem(me + k, n), me).start()
        return carry

    lax.fori_loop(1, n, send_blade, 0)
    arrived[me] = blocks[me // per]

    @pl.when(jnp.logical_not(has_high))
    def _():
        u[:, cx + 2 : cx + 4] = jnp.zeros((3, 2) + u.shape[2:], jnp.float32)
        prov[0, cx + 1] = jnp.zeros(prov.shape[2:], jnp.float32)
        p1[cx + 4 : cx + 6] = jnp.zeros((2,) + p1.shape[1:], jnp.float32)
        part_in[1] = jnp.zeros(part_in.shape[1:], jnp.float32)

    @pl.when(jnp.logical_not(has_low))
    def _():
        prov[0, 0] = jnp.zeros(prov.shape[2:], jnp.float32)
        p1[0:2] = jnp.zeros((2,) + p1.shape[1:], jnp.float32)
        part_in[0] = jnp.zeros(part_in.shape[1:], jnp.float32)

    def wrap(ref, *lead):
        ref[(*lead, slice(PAD - 1, PAD))] = ref[(*lead, slice(PAD + ny - 1, PAD + ny))]
        ref[(*lead, slice(PAD + ny, PAD + ny + 1))] = ref[(*lead, slice(PAD, PAD + 1))]

    load.wait()
    for i in range(3):
        for x in range(cx):
            wrap(u, i, x + 2)

    depth_bits, span_bits = nz.bit_length() - 1, ny.bit_length() - 1
    layer = lax.broadcasted_iota(jnp.int32, (LANES, 256), 0)

    def weights(q):
        info = table[q]
        where = (info[0:1] + 0.5).astype(jnp.int32) - 1
        full = where >= 0
        a = where >> (depth_bits + span_bits)
        b = (where >> depth_bits) & (ny - 1)
        d = where & (nz - 1)
        fx, fy, fz = info[1:2], info[2:3], info[3:4]
        along_z = jnp.where(layer == d, 1.0 - fz, jnp.where(layer == d + 1, fz, 0.0))
        next_b = (b + 1) & (ny - 1)
        along_y = jnp.where(layer == b, 1.0 - fy, jnp.where(layer == next_b, fy, 0.0))
        along_x = []
        for x in range(cx):
            kept = jnp.where(a == x, 1.0 - fx, jnp.where(a + 1 == x, fx, 0.0))
            along_x.append(jnp.where(full, kept, 0.0))
        return along_x, along_y, split(along_z)

    sampled = []
    for q in range(chunks):
        along_x, along_y, along_z = weights(q)
        for i in range(3):
            total = jnp.zeros((1, 256), jnp.float32)
            for x in range(cx):
                lines = product(split(u[i, x + 2, body]), along_z, ((1,), (0,)))
                total = total + along_x[x] * jnp.sum(lines * along_y, axis=0, keepdims=True)
            sampled.append(total)

    def take_blade(k, carry):
        blade(k, me, lax.rem(me + n - k, n)).wait_recv()
        return carry

    lax.fori_loop(1, n, take_blade, 0)
    lane = lax.broadcasted_iota(jnp.int32, (8, LANES), 1)
    mine = lax.rem(me, per)
    for q in range(chunks):
        halves = []
        for h in range(256 // LANES):
            block = jnp.zeros((8, LANES), jnp.float32)
            for o in range(per):
                shift = lax.rem(o - mine + per, per) * SLOT
                moved = pltpu.roll(arrived[(q * (256 // LANES) + h) * per + o], shift, 1)
                block = jnp.where((lane >> 4) == o, moved, block)
            halves.append(block)
        point = jnp.concatenate(halves, axis=1)
        along_x, along_y, along_z = weights(q)
        r = [sampled[3 * q + i] - point[i : i + 1] for i in range(3)]
        e = [point[3 + i : 4 + i] for i in range(3)]
        speed = jnp.sqrt(r[0] * r[0] + r[1] * r[1] + r[2] * r[2] + STRAIN_FLOOR)
        size = (TIME_STEP * FORCE_SCALE) * point[6:7] * speed
        lift = [
            r[1] * e[2] - r[2] * e[1],
            r[2] * e[0] - r[0] * e[2],
            r[0] * e[1] - r[1] * e[0],
        ]
        for i in range(3):
            force = size * (lift[i] - r[i])
            for x in range(cx):
                laid = product(
                    split(along_y * (force * along_x[x])), along_z, ((1,), (1,))
                )
                if q == 0:
                    prov[i, x + 1, body] = laid
                else:
                    prov[i, x + 1, body] += laid

    @pl.when(has_low)
    def _():
        halo(True).wait_recv()

    @pl.when(has_high)
    def _():
        halo(False).wait_recv()

    @pl.when(jnp.logical_not(has_low))
    def _():
        def take_inlet(k, carry):
            feed(k).wait_recv()
            return carry

        lax.fori_loop(1, n, take_inlet, 0)
        inlet[0] = inflow[...]
        share = inflow.shape[1]
        for k in range(n):
            at = slice(PAD + k * share, PAD + (k + 1) * share)
            for i in range(3):
                u[i, 0, at] = inlet[k, i]
                u[i, 1, at] = inlet[k, i]

    for i in range(3):
        wrap(u, i, 1)
        wrap(u, i, cx + 2)

    first = lax.broadcasted_iota(jnp.int32, (ROWS, nz), 1) == 0
    last = lax.broadcasted_iota(jnp.int32, (ROWS, nz), 1) == nz - 1

    def deeper(value, edge=0.0):
        return jnp.where(last, edge, pltpu.roll(value, nz - 1, 1))

    def shallower(value, edge=0.0):
        return jnp.where(first, edge, pltpu.roll(value, 1, 1))

    starts = range(PAD, PAD + ny, ROWS)

    def at(start, shift=0):
        return pl.ds(start + shift, ROWS)

    def viscosity(p, carry):
        for s in starts:
            d = []
            for i in range(3):
                centre = u[i, p + 1, at(s)]
                d.append(
                    (
                        u[i, p + 2, at(s)] - u[i, p, at(s)],
                        u[i, p + 1, at(s, 1)] - u[i, p + 1, at(s, -1)],
                        deeper(centre) - shallower(centre),
                    )
                )
            xy, xz, yz = d[0][1] + d[1][0], d[0][2] + d[2][0], d[1][2] + d[2][1]
            shear = d[0][0] * d[0][0] + d[1][1] * d[1][1] + d[2][2] * d[2][2]
            shear = shear + shear + (xy * xy + xz * xz + yz * yz) + 4.0 * STRAIN_FLOOR
            nu[p, at(s)] = (0.25 * TIME_STEP * SMAGORINSKY) * jnp.sqrt(shear)
        wrap(nu, p)
        return carry

    lax.fori_loop(0, cx + 2, viscosity, 0)

    def momentum(p, carry):
        for s in starts:
            centre = [u[i, p + 2, at(s)] for i in range(3)]
            own = nu[p + 1, at(s)]
            edge = centre[2] * centre[2]
            edge = edge + edge + centre[0] * centre[0] + centre[1] * centre[1]
            edge = (0.25 * TIME_STEP * SMAGORINSKY) * jnp.sqrt(edge + 4.0 * STRAIN_FLOOR)
            carried = [(0.5 * TIME_STEP) * value for value in centre]
            coef = [
                own + nu[p + 2, at(s)] - carried[0],
                own + nu[p, at(s)] + carried[0],
                own + nu[p + 1, at(s, 1)] - carried[1],
                own + nu[p + 1, at(s, -1)] + carried[1],
                own + deeper(own, edge) - carried[2],
                own + shallower(own, edge) + carried[2],
            ]
            rest = 1.0 - (coef[0] + coef[1] + coef[2] + coef[3] + coef[4] + coef[5])
            for i in range(3):
                value = prov[i, p + 1, at(s)] + rest * centre[i]
                value = value + coef[0] * u[i, p + 3, at(s)] + coef[1] * u[i, p + 1, at(s)]
                value = value + coef[2] * u[i, p + 2, at(s, 1)] + coef[3] * u[i, p + 2, at(s, -1)]
                value = value + coef[4] * deeper(centre[i]) + coef[5] * shallower(centre[i])
                prov[i, p + 1, at(s)] = value
        wrap(prov, 1, p + 1)
        return carry

    lax.fori_loop(0, cx, momentum, 0)

    scale = -1.0 / 12.0

    def flat_part(p, s):
        w = prov[2, p + 1, at(s)]
        return prov[1, p + 1, at(s, 1)] - prov[1, p + 1, at(s, -1)] + deeper(w) - shallower(w)

    def rim(up, what):
        if what == 0:
            src = prov.at[0, cx if up else 1, body]
            dst = prov.at[0, 0 if up else cx + 1, body]
        elif what == 1:
            src = part_out.at[1 if up else 0]
            dst = part_in.at[0 if up else 1]
        else:
            src = p1.at[cx : cx + 2, body] if up else p1.at[4:6, body]
            dst = p1.at[0:2, body] if up else p1.at[cx + 4 : cx + 6, body]
        k = 3 * int(up) + what
        return pltpu.make_async_remote_copy(
            src_ref=src,
            dst_ref=dst,
            send_sem=rim_send.at[k],
            recv_sem=rim_recv.at[k],
            device_id={"gx": me + 1 if up else me - 1},
            device_id_type=MESH,
        )

    def send_rim(what):
        @pl.when(has_low)
        def _():
            rim(False, what).start()

        @pl.when(has_high)
        def _():
            rim(True, what).start()

    send_rim(0)
    for s in starts:
        o = pl.ds(s - PAD, ROWS)
        part_out[0, o] = scale * (flat_part(0, s) + prov[0, 2, at(s)])
        part_out[1, o] = scale * (flat_part(cx - 1, s) - prov[0, cx - 1, at(s)])
    send_rim(1)
    for p in range(1, cx - 1):
        for s in starts:
            p1[p + 3, at(s)] = scale * (
                flat_part(p, s) + prov[0, p + 2, at(s)] - prov[0, p, at(s)]
            )
    send_rim(2)
    for p in range(1, cx - 1):
        wrap(p1, p + 3)

    for what in range(3):

        @pl.when(has_low)
        def _():
            rim(True, what).wait_recv()

        @pl.when(has_high)
        def _():
            rim(False, what).wait_recv()

    for s in starts:
        o = pl.ds(s - PAD, ROWS)
        p1[3, at(s)] = part_out[0, o] - scale * prov[0, 0, at(s)]
        p1[cx + 2, at(s)] = part_out[1, o] + scale * prov[0, cx + 1, at(s)]
        p1[2, at(s)] = low_ok * (part_in[0, o] + scale * prov[0, 1, at(s)])
        p1[cx + 3, at(s)] = high_ok * (part_in[1, o] - scale * prov[0, cx, at(s)])
    for p in (1, 2, 3, cx + 2, cx + 3, cx + 4):
        wrap(p1, p)

    def sweep(old, new, back):
        planes = new.shape[0]
        outer = (planes - cx) // 2

        def plane(p, carry):
            ok = jnp.where(p < outer, low_ok, jnp.where(p >= outer + cx, high_ok, 1.0))
            for s in starts:
                centre = old[p + 1, at(s)]
                near = old[p, at(s)] + old[p + 2, at(s)]
                near = near + old[p + 1, at(s, 1)] + old[p + 1, at(s, -1)]
                near = near + deeper(centre) + shallower(centre)
                new[p, at(s)] = ok * (near * (1.0 / 6.0) + p1[p + back, at(s)])
            wrap(new, p)
            return carry

        lax.fori_loop(0, planes, plane, 0)

    sweep(p1, p2, 1)
    sweep(p2, p3, 2)

    def correct(p, carry):
        for s in starts:
            o = pl.ds(s - PAD, ROWS)
            centre = p3[p + 1, at(s)]
            out[0, p, o] = prov[0, p + 1, at(s)] - 0.5 * (p3[p + 2, at(s)] - p3[p, at(s)])
            out[1, p, o] = prov[1, p + 1, at(s)] - 0.5 * (
                p3[p + 1, at(s, 1)] - p3[p + 1, at(s, -1)]
            )
            out[2, p, o] = prov[2, p + 1, at(s)] - 0.5 * (deeper(centre) - shallower(centre))
        return carry

    lax.fori_loop(0, cx, correct, 0)

    def sent_blade(k, carry):
        blade(k, lax.rem(me + k, n), me).wait_send()
        return carry

    lax.fori_loop(1, n, sent_blade, 0)

    @pl.when(has_low)
    def _():
        feed(me).wait_send()
        halo(False).wait_send()
        for what in range(3):
            rim(False, what).wait_send()

    @pl.when(has_high)
    def _():
        halo(True).wait_send()
        for what in range(3):
            rim(True, what).wait_send()


def shards(n, velocity, inflow, blade_motion, blade_axis, blade_chord, host_cell, host_frac):
    cx, ny, nz = velocity.shape[1:]
    slots = host_cell.shape[0]
    high = PAD + ny + 8
    vmem = pltpu.VMEM
    f32 = jnp.float32
    dma = pltpu.SemaphoreType.DMA
    inside = pl.BlockSpec(memory_space=pltpu.VMEM)
    return pl.pallas_call(
        functools.partial(kernel, n),
        out_shape=jax.ShapeDtypeStruct(velocity.shape, f32),
        in_specs=[pl.BlockSpec(memory_space=pl.ANY)] + [inside] * 6,
        out_specs=inside,
        scratch_shapes=[
            vmem((3, cx + 4, high, nz), f32),
            vmem((cx + 2, high, nz), f32),
            vmem((3, cx + 2, high, nz), f32),
            vmem((cx + 6, high, nz), f32),
            vmem((cx + 4, high, nz), f32),
            vmem((cx + 2, high, nz), f32),
            vmem((2, ny, nz), f32),
            vmem((2, ny, nz), f32),
            vmem((16, slots), f32),
            vmem((n * SLOT // LANES, 8, LANES), f32),
            vmem((n * SLOT // 256, 8, 256), f32),
            vmem((n, 8, LANES), f32),
            vmem((n,) + inflow.shape, f32),
            dma,
            dma((2,)),
            dma((2,)),
            dma((n,)),
            dma((n,)),
            dma,
            dma((n,)),
            dma((6,)),
            dma((6,)),
        ],
        compiler_params=pltpu.CompilerParams(
            collective_id=0, has_side_effects=True, vmem_limit_bytes=48 * 1024 * 1024
        ),
    )(
        velocity,
        inflow,
        blade_motion,
        blade_axis,
        blade_chord.reshape(1, slots),
        host_cell.reshape(1, slots),
        host_frac,
    )


def solution(mesh):
    return jax.shard_map(
        functools.partial(shards, mesh.shape["gx"]),
        mesh=mesh,
        in_specs=(
            P("runs", "gx", None, None),
            P("runs", "gx", None),
            P("runs", "gx"),
            P("runs", "gx"),
            P(("runs", "gx")),
            P(("runs", "gx")),
            P("runs", "gx"),
        ),
        out_specs=P("runs", "gx", None, None),
        check_vma=False,
    )
```

```python
import functools

import jax
import jax.numpy as jnp
from jax import lax
from jax.experimental import pallas as pl
from jax.experimental.pallas import tpu as pltpu
from jax.sharding import PartitionSpec as P

TIME_STEP = 0.2
SMAGORINSKY = 0.0289
STRAIN_FLOOR = 0.01
FORCE_SCALE = 0.2

MESH = pl.DeviceIdType.MESH
PAD = 8
ROWS = 16
SLOT = 16
LANES = 128


def split(value):
    high = value.astype(jnp.bfloat16)
    return high, (value - high.astype(jnp.float32)).astype(jnp.bfloat16)


def product(left, right, contract):
    def one(a, b):
        return lax.dot_general(
            a, b, (contract, ((), ())), preferred_element_type=jnp.float32
        )

    return one(left[0], right[0]) + (one(left[0], right[1]) + one(left[1], right[0]))


def kernel(
    n,
    vel,
    inflow,
    motion,
    axis,
    chord,
    cell,
    frac,
    out,
    motion_in,
    axis_in,
    chord_in,
    cell_in,
    frac_in,
    u,
    nu,
    prov,
    p1,
    p2,
    p3,
    part_out,
    part_in,
    rows,
    blocks,
    table,
    arrived,
    inlet,
    load_sem,
    small_sem,
    own_sem,
    halo_send,
    halo_recv,
    blade_send,
    blade_recv,
    in_send,
    in_recv,
    nu_send,
    nu_recv,
    rim_send,
    rim_recv,
    result,
    store_sem,
):
    me = lax.axis_index("gx")
    cx, ny, nz = vel.shape[1:]
    cap = cell.shape[1] // n
    body = pl.ds(PAD, ny)
    has_low, has_high = me > 0, me < n - 1
    low_ok = jnp.where(has_low, 1.0, 0.0)
    high_ok = jnp.where(has_high, 1.0, 0.0)

    barrier = pltpu.get_barrier_semaphore()

    def greet(k, carry):
        pl.semaphore_signal(
            barrier, inc=1, device_id={"gx": lax.rem(me + k, n)}, device_id_type=MESH
        )
        return carry

    lax.fori_loop(1, n, greet, 0)
    pairs = (
        (motion, motion_in),
        (axis, axis_in),
        (chord, chord_in),
        (cell, cell_in),
        (frac, frac_in),
    )
    small = [pltpu.make_async_copy(a, b, small_sem.at[k]) for k, (a, b) in enumerate(pairs)]
    for copy in small:
        copy.start()
    load = pltpu.make_async_copy(vel, u.at[:, 1 : 1 + cx, body], load_sem)
    load.start()

    zeros = jnp.zeros((16, rows.shape[1]), jnp.float32)
    rows[...] = zeros
    owners = 256 // SLOT
    wide = owners * cap
    source_lane = lax.broadcasted_iota(jnp.int32, (wide, 256), 0)
    slot_lane = lax.broadcasted_iota(jnp.int32, (wide, 256), 1)
    within = slot_lane & (SLOT - 1)
    picked = (source_lane == (slot_lane >> 4) * cap + within) & (within < cap)
    pick = jnp.where(picked, 1.0, 0.0)
    chunks = n // owners
    for copy in small:
        copy.wait()
    rows[0:3] = motion_in[...]
    rows[3:6] = axis_in[...]
    rows[6:7] = chord_in[...]
    rows[8:9] = (cell_in[...] + 1).astype(jnp.float32)
    rows[9:12] = frac_in[...]
    for q in range(chunks):
        spaced = lax.dot_general(
            rows[:, q * wide : (q + 1) * wide],
            pick,
            (((1,), (0,)), ((), ())),
            precision=lax.Precision.HIGHEST,
            preferred_element_type=jnp.float32,
        )
        table[q] = spaced[8:16]
        for h in range(256 // LANES):
            blocks[q * (256 // LANES) + h] = spaced[0:8, h * LANES : (h + 1) * LANES]

    def halo(up):
        if up:
            src, dst, to = vel.at[:, cx - 1], u.at[:, 0, body], me + 1
        else:
            src, dst, to = vel.at[:, 0], u.at[:, cx + 1, body], me - 1
        return pltpu.make_async_remote_copy(
            src_ref=src,
            dst_ref=dst,
            send_sem=halo_send.at[int(up)],
            recv_sem=halo_recv.at[int(up)],
            device_id={"gx": to},
            device_id_type=MESH,
        )

    per = LANES // SLOT

    def blade(k, to, slot):
        return pltpu.make_async_remote_copy(
            src_ref=blocks.at[to // per],
            dst_ref=arrived.at[slot],
            send_sem=blade_send.at[k],
            recv_sem=blade_recv.at[k],
            device_id={"gx": to},
            device_id_type=MESH,
        )

    def feed(slot):
        return pltpu.make_async_remote_copy(
            src_ref=inflow,
            dst_ref=inlet.at[slot],
            send_sem=in_send,
            recv_sem=in_recv.at[slot],
            device_id={"gx": 0},
            device_id_type=MESH,
        )

    pl.semaphore_wait(barrier, n - 1)

    @pl.when(has_low)
    def _():
        feed(me).start()
        halo(False).start()

    @pl.when(has_high)
    def _():
        halo(True).start()

    def send_blade(k, carry):
        blade(k, lax.rem(me + k, n), me).start()
        return carry

    lax.fori_loop(1, n, send_blade, 0)
    arrived[me] = blocks[me // per]

    @pl.when(jnp.logical_not(has_high))
    def _():
        u[:, cx + 1] = jnp.zeros((3,) + u.shape[2:], jnp.float32)
        prov[0, cx + 1] = jnp.zeros(prov.shape[2:], jnp.float32)
        p1[cx + 4 : cx + 6] = jnp.zeros((2,) + p1.shape[1:], jnp.float32)
        part_in[1] = jnp.zeros(part_in.shape[1:], jnp.float32)

    @pl.when(jnp.logical_not(has_low))
    def _():
        prov[0, 0] = jnp.zeros(prov.shape[2:], jnp.float32)
        p1[0:2] = jnp.zeros((2,) + p1.shape[1:], jnp.float32)
        part_in[0] = jnp.zeros(part_in.shape[1:], jnp.float32)

    def wrap(ref, *lead):
        ref[(*lead, slice(PAD - 1, PAD))] = ref[(*lead, slice(PAD + ny - 1, PAD + ny))]
        ref[(*lead, slice(PAD + ny, PAD + ny + 1))] = ref[(*lead, slice(PAD, PAD + 1))]

    load.wait()
    for i in range(3):
        for x in range(cx):
            wrap(u, i, x + 1)

    depth_bits, span_bits = nz.bit_length() - 1, ny.bit_length() - 1
    layer = lax.broadcasted_iota(jnp.int32, (LANES, 256), 0)

    def weights(q):
        info = table[q]
        where = (info[0:1] + 0.5).astype(jnp.int32) - 1
        full = where >= 0
        a = where >> (depth_bits + span_bits)
        b = (where >> depth_bits) & (ny - 1)
        d = where & (nz - 1)
        fx, fy, fz = info[1:2], info[2:3], info[3:4]
        along_z = jnp.where(layer == d, 1.0 - fz, jnp.where(layer == d + 1, fz, 0.0))
        next_b = (b + 1) & (ny - 1)
        along_y = jnp.where(layer == b, 1.0 - fy, jnp.where(layer == next_b, fy, 0.0))
        along_x = []
        for x in range(cx):
            kept = jnp.where(a == x, 1.0 - fx, jnp.where(a + 1 == x, fx, 0.0))
            along_x.append(jnp.where(full, kept, 0.0))
        return along_x, along_y, split(along_z)

    sampled = []
    for q in range(chunks):
        along_x, along_y, along_z = weights(q)
        for i in range(3):
            total = jnp.zeros((1, 256), jnp.float32)
            for x in range(cx):
                lines = product(split(u[i, x + 1, body]), along_z, ((1,), (0,)))
                total = total + along_x[x] * jnp.sum(lines * along_y, axis=0, keepdims=True)
            sampled.append(total)

    def take_blade(k, carry):
        blade(k, me, lax.rem(me + n - k, n)).wait_recv()
        return carry

    lax.fori_loop(1, n, take_blade, 0)
    lane = lax.broadcasted_iota(jnp.int32, (8, LANES), 1)
    mine = lax.rem(me, per)
    for q in range(chunks):
        halves = []
        for h in range(256 // LANES):
            block = jnp.zeros((8, LANES), jnp.float32)
            for o in range(per):
                shift = lax.rem(o - mine + per, per) * SLOT
                moved = pltpu.roll(arrived[(q * (256 // LANES) + h) * per + o], shift, 1)
                block = jnp.where((lane >> 4) == o, moved, block)
            halves.append(block)
        point = jnp.concatenate(halves, axis=1)
        along_x, along_y, along_z = weights(q)
        r = [sampled[3 * q + i] - point[i : i + 1] for i in range(3)]
        e = [point[3 + i : 4 + i] for i in range(3)]
        speed = jnp.sqrt(r[0] * r[0] + r[1] * r[1] + r[2] * r[2] + STRAIN_FLOOR)
        size = (TIME_STEP * FORCE_SCALE) * point[6:7] * speed
        lift = [
            r[1] * e[2] - r[2] * e[1],
            r[2] * e[0] - r[0] * e[2],
            r[0] * e[1] - r[1] * e[0],
        ]
        for i in range(3):
            force = size * (lift[i] - r[i])
            for x in range(cx):
                laid = product(
                    split(along_y * (force * along_x[x])), along_z, ((1,), (1,))
                )
                if q == 0:
                    prov[i, x + 1, body] = laid
                else:
                    prov[i, x + 1, body] += laid

    first = lax.broadcasted_iota(jnp.int32, (ROWS, nz), 1) == 0
    last = lax.broadcasted_iota(jnp.int32, (ROWS, nz), 1) == nz - 1

    def deeper(value, edge=0.0):
        return jnp.where(last, edge, pltpu.roll(value, nz - 1, 1))

    def shallower(value, edge=0.0):
        return jnp.where(first, edge, pltpu.roll(value, 1, 1))

    starts = range(PAD, PAD + ny, ROWS)

    def at(start, shift=0):
        return pl.ds(start + shift, ROWS)

    def viscosity(p, low, mid, up):
        for s in starts:
            d = []
            for i in range(3):
                centre = u[i, mid, at(s)]
                d.append(
                    (
                        u[i, up, at(s)] - u[i, low, at(s)],
                        u[i, mid, at(s, 1)] - u[i, mid, at(s, -1)],
                        deeper(centre) - shallower(centre),
                    )
                )
            xy, xz, yz = d[0][1] + d[1][0], d[0][2] + d[2][0], d[1][2] + d[2][1]
            shear = d[0][0] * d[0][0] + d[1][1] * d[1][1] + d[2][2] * d[2][2]
            shear = shear + shear + (xy * xy + xz * xz + yz * yz) + 4.0 * STRAIN_FLOOR
            nu[p, at(s)] = (0.25 * TIME_STEP * SMAGORINSKY) * jnp.sqrt(shear)
        wrap(nu, p)

    def inner_viscosity(p, carry):
        viscosity(p + 1, p, p + 1, p + 2)
        return carry

    lax.fori_loop(1, cx - 1, inner_viscosity, 0)

    @pl.when(has_low)
    def _():
        halo(True).wait_recv()

    @pl.when(has_high)
    def _():
        halo(False).wait_recv()

    @pl.when(jnp.logical_not(has_low))
    def _():
        def take_inlet(k, carry):
            feed(k).wait_recv()
            return carry

        lax.fori_loop(1, n, take_inlet, 0)
        own = pltpu.make_async_copy(inflow, inlet.at[0], own_sem)
        own.start()
        own.wait()
        share = inflow.shape[1]
        for k in range(n):
            at = slice(PAD + k * share, PAD + (k + 1) * share)
            for i in range(3):
                u[i, 0, at] = inlet[k, i]

    for i in range(3):
        wrap(u, i, 0)
        wrap(u, i, cx + 1)

    def layer_of(up):
        return pltpu.make_async_remote_copy(
            src_ref=nu.at[cx if up else 1, body],
            dst_ref=nu.at[0 if up else cx + 1, body],
            send_sem=nu_send.at[int(up)],
            recv_sem=nu_recv.at[int(up)],
            device_id={"gx": me + 1 if up else me - 1},
            device_id_type=MESH,
        )

    viscosity(1, 0, 1, 2)

    @pl.when(has_low)
    def _():
        layer_of(False).start()

    viscosity(cx, cx - 1, cx, cx + 1)

    @pl.when(has_high)
    def _():
        layer_of(True).start()

    @pl.when(jnp.logical_not(has_low))
    def _():
        viscosity(0, 0, 0, 1)

    @pl.when(jnp.logical_not(has_high))
    def _():
        viscosity(cx + 1, cx, cx + 1, cx + 1)

    def momentum(p):
        for s in starts:
            centre = [u[i, p + 1, at(s)] for i in range(3)]
            own = nu[p + 1, at(s)]
            edge = centre[2] * centre[2]
            edge = edge + edge + centre[0] * centre[0] + centre[1] * centre[1]
            edge = (0.25 * TIME_STEP * SMAGORINSKY) * jnp.sqrt(edge + 4.0 * STRAIN_FLOOR)
            carried = [(0.5 * TIME_STEP) * value for value in centre]
            coef = [
                own + nu[p + 2, at(s)] - carried[0],
                own + nu[p, at(s)] + carried[0],
                own + nu[p + 1, at(s, 1)] - carried[1],
                own + nu[p + 1, at(s, -1)] + carried[1],
                own + deeper(own, edge) - carried[2],
                own + shallower(own, edge) + carried[2],
            ]
            rest = 1.0 - (coef[0] + coef[1] + coef[2] + coef[3] + coef[4] + coef[5])
            for i in range(3):
                value = prov[i, p + 1, at(s)] + rest * centre[i]
                value = value + coef[0] * u[i, p + 2, at(s)] + coef[1] * u[i, p, at(s)]
                value = value + coef[2] * u[i, p + 1, at(s, 1)] + coef[3] * u[i, p + 1, at(s, -1)]
                value = value + coef[4] * deeper(centre[i]) + coef[5] * shallower(centre[i])
                prov[i, p + 1, at(s)] = value
        wrap(prov, 1, p + 1)

    def inner_momentum(p, carry):
        momentum(p)
        return carry

    lax.fori_loop(1, cx - 1, inner_momentum, 0)

    scale = -1.0 / 12.0

    def flat_part(p, s):
        w = prov[2, p + 1, at(s)]
        return prov[1, p + 1, at(s, 1)] - prov[1, p + 1, at(s, -1)] + deeper(w) - shallower(w)

    def rim(up, what):
        if what == 0:
            src = prov.at[0, cx if up else 1, body]
            dst = prov.at[0, 0 if up else cx + 1, body]
        elif what == 1:
            src = part_out.at[1 if up else 0]
            dst = part_in.at[0 if up else 1]
        else:
            plane = cx - 5 + what if up else what - 1
            src = p1.at[plane + 3, body]
            dst = p1.at[plane + 3 - cx if up else plane + 3 + cx, body]
        k = 4 * int(up) + what
        return pltpu.make_async_remote_copy(
            src_ref=src,
            dst_ref=dst,
            send_sem=rim_send.at[k],
            recv_sem=rim_recv.at[k],
            device_id={"gx": me + 1 if up else me - 1},
            device_id_type=MESH,
        )

    def send_rim(up, what):
        @pl.when(has_high if up else has_low)
        def _():
            rim(up, what).start()

    def first_potential(p):
        for s in starts:
            p1[p + 3, at(s)] = scale * (
                flat_part(p, s) + prov[0, p + 2, at(s)] - prov[0, p, at(s)]
            )

    @pl.when(has_low)
    def _():
        layer_of(True).wait_recv()

    momentum(0)
    send_rim(False, 0)
    for s in starts:
        part_out[0, pl.ds(s - PAD, ROWS)] = scale * (flat_part(0, s) + prov[0, 2, at(s)])
    send_rim(False, 1)
    for p in range(1, cx - 2):
        first_potential(p)
    send_rim(False, 2)
    send_rim(True, 2)

    @pl.when(has_high)
    def _():
        layer_of(False).wait_recv()

    momentum(cx - 1)
    send_rim(True, 0)
    for s in starts:
        part_out[1, pl.ds(s - PAD, ROWS)] = scale * (
            flat_part(cx - 1, s) - prov[0, cx - 1, at(s)]
        )
    send_rim(True, 1)
    first_potential(cx - 2)
    send_rim(False, 3)
    send_rim(True, 3)
    for p in range(1, cx - 1):
        wrap(p1, p + 3)

    for what in range(4):

        @pl.when(has_low)
        def _():
            rim(True, what).wait_recv()

        @pl.when(has_high)
        def _():
            rim(False, what).wait_recv()

    for s in starts:
        o = pl.ds(s - PAD, ROWS)
        p1[3, at(s)] = part_out[0, o] - scale * prov[0, 0, at(s)]
        p1[cx + 2, at(s)] = part_out[1, o] + scale * prov[0, cx + 1, at(s)]
        p1[2, at(s)] = low_ok * (part_in[0, o] + scale * prov[0, 1, at(s)])
        p1[cx + 3, at(s)] = high_ok * (part_in[1, o] - scale * prov[0, cx, at(s)])
    for p in (1, 2, 3, cx + 2, cx + 3, cx + 4):
        wrap(p1, p)

    def sweep(old, new, back):
        planes = new.shape[0]
        outer = (planes - cx) // 2

        def plane(p, carry):
            ok = jnp.where(p < outer, low_ok, jnp.where(p >= outer + cx, high_ok, 1.0))
            for s in starts:
                centre = old[p + 1, at(s)]
                near = old[p, at(s)] + old[p + 2, at(s)]
                near = near + old[p + 1, at(s, 1)] + old[p + 1, at(s, -1)]
                near = near + deeper(centre) + shallower(centre)
                new[p, at(s)] = ok * (near * (1.0 / 6.0) + p1[p + back, at(s)])
            wrap(new, p)
            return carry

        lax.fori_loop(0, planes, plane, 0)

    sweep(p1, p2, 1)
    sweep(p2, p3, 2)

    def store(p):
        return pltpu.make_async_copy(result.at[:, p], out.at[:, p], store_sem.at[p])

    def correct(p, carry):
        for s in starts:
            o = pl.ds(s - PAD, ROWS)
            centre = p3[p + 1, at(s)]
            result[0, p, o] = prov[0, p + 1, at(s)] - 0.5 * (p3[p + 2, at(s)] - p3[p, at(s)])
            result[1, p, o] = prov[1, p + 1, at(s)] - 0.5 * (
                p3[p + 1, at(s, 1)] - p3[p + 1, at(s, -1)]
            )
            result[2, p, o] = prov[2, p + 1, at(s)] - 0.5 * (deeper(centre) - shallower(centre))
        store(p).start()
        return carry

    lax.fori_loop(0, cx, correct, 0)

    def sent_blade(k, carry):
        blade(k, lax.rem(me + k, n), me).wait_send()
        return carry

    lax.fori_loop(1, n, sent_blade, 0)
    for p in range(cx):
        store(p).wait()

    @pl.when(has_low)
    def _():
        feed(me).wait_send()
        halo(False).wait_send()
        layer_of(False).wait_send()
        for what in range(4):
            rim(False, what).wait_send()

    @pl.when(has_high)
    def _():
        halo(True).wait_send()
        layer_of(True).wait_send()
        for what in range(4):
            rim(True, what).wait_send()


def shards(n, velocity, inflow, blade_motion, blade_axis, blade_chord, host_cell, host_frac):
    cx, ny, nz = velocity.shape[1:]
    slots = host_cell.shape[0]
    high = PAD + ny + 8
    vmem = pltpu.VMEM
    f32 = jnp.float32
    dma = pltpu.SemaphoreType.DMA
    return pl.pallas_call(
        functools.partial(kernel, n),
        out_shape=jax.ShapeDtypeStruct(velocity.shape, f32),
        in_specs=[pl.BlockSpec(memory_space=pltpu.HBM)] * 7,
        out_specs=pl.BlockSpec(memory_space=pltpu.HBM),
        scratch_shapes=[
            vmem((3, slots), f32),
            vmem((3, slots), f32),
            vmem((1, slots), f32),
            vmem((1, slots), jnp.int32),
            vmem((3, slots), f32),
            vmem((3, cx + 2, high, nz), f32),
            vmem((cx + 2, high, nz), f32),
            vmem((3, cx + 2, high, nz), f32),
            vmem((cx + 6, high, nz), f32),
            vmem((cx + 4, high, nz), f32),
            vmem((cx + 2, high, nz), f32),
            vmem((2, ny, nz), f32),
            vmem((2, ny, nz), f32),
            vmem((16, slots), f32),
            vmem((n * SLOT // LANES, 8, LANES), f32),
            vmem((n * SLOT // 256, 8, 256), f32),
            vmem((n, 8, LANES), f32),
            vmem((n,) + inflow.shape, f32),
            dma,
            dma((5,)),
            dma,
            dma((2,)),
            dma((2,)),
            dma((n,)),
            dma((n,)),
            dma,
            dma((n,)),
            dma((2,)),
            dma((2,)),
            dma((8,)),
            dma((8,)),
            vmem(velocity.shape, f32),
            dma((cx,)),
        ],
        compiler_params=pltpu.CompilerParams(
            collective_id=0, has_side_effects=True, vmem_limit_bytes=64 * 1024 * 1024 - 65536
        ),
    )(
        velocity,
        inflow,
        blade_motion,
        blade_axis,
        blade_chord.reshape(1, slots),
        host_cell.reshape(1, slots),
        host_frac,
    )


def solution(mesh):
    return jax.shard_map(
        functools.partial(shards, mesh.shape["gx"]),
        mesh=mesh,
        in_specs=(
            P("runs", "gx", None, None),
            P("runs", "gx", None),
            P("runs", "gx"),
            P("runs", "gx"),
            P(("runs", "gx")),
            P(("runs", "gx")),
            P("runs", "gx"),
        ),
        out_specs=P("runs", "gx", None, None),
        check_vma=False,
    )
```

```python
import functools

import jax
import jax.numpy as jnp
from jax import lax
from jax.experimental import pallas as pl
from jax.experimental.pallas import tpu as pltpu
from jax.sharding import PartitionSpec as P

TIME_STEP = 0.2
SMAGORINSKY = 0.0289
STRAIN_FLOOR = 0.01
FORCE_SCALE = 0.2

MESH = pl.DeviceIdType.MESH
PAD = 8
ROWS = 16
SLOT = 16
LANES = 128


def split(value):
    high = value.astype(jnp.bfloat16)
    return high, (value - high.astype(jnp.float32)).astype(jnp.bfloat16)


def product(left, right, contract):
    def one(a, b):
        return lax.dot_general(
            a, b, (contract, ((), ())), preferred_element_type=jnp.float32
        )

    return one(left[0], right[0]) + (one(left[0], right[1]) + one(left[1], right[0]))


def kernel(
    n,
    vel,
    inflow,
    motion,
    axis,
    chord,
    cell,
    frac,
    given,
    change,
    motion_in,
    axis_in,
    chord_in,
    cell_in,
    frac_in,
    u,
    nu,
    prov,
    p1,
    p2,
    p3,
    part_out,
    part_in,
    rows,
    blocks,
    table,
    arrived,
    inlet,
    load_sem,
    small_sem,
    own_sem,
    halo_send,
    halo_recv,
    blade_send,
    blade_recv,
    in_send,
    in_recv,
    nu_send,
    nu_recv,
    rim_send,
    rim_recv,
    result,
    keep_sem,
    store_sem,
):
    me = lax.axis_index("gx")
    cx, ny, nz = vel.shape[1:]
    cap = cell.shape[1] // n
    body = pl.ds(PAD, ny)
    has_low, has_high = me > 0, me < n - 1
    low_ok = jnp.where(has_low, 1.0, 0.0)
    high_ok = jnp.where(has_high, 1.0, 0.0)

    barrier = pltpu.get_barrier_semaphore()

    def greet(k, carry):
        pl.semaphore_signal(
            barrier, inc=1, device_id={"gx": lax.rem(me + k, n)}, device_id_type=MESH
        )
        return carry

    lax.fori_loop(1, n, greet, 0)
    pairs = (
        (motion, motion_in),
        (axis, axis_in),
        (chord, chord_in),
        (cell, cell_in),
        (frac, frac_in),
    )
    small = [pltpu.make_async_copy(a, b, small_sem.at[k]) for k, (a, b) in enumerate(pairs)]
    for copy in small:
        copy.start()
    load = pltpu.make_async_copy(vel, u.at[:, 1 : 1 + cx, body], load_sem)
    load.start()

    def halo(up):
        if up:
            src, dst, to = vel.at[:, cx - 1], u.at[:, 0, body], me + 1
        else:
            src, dst, to = vel.at[:, 0], u.at[:, cx + 1, body], me - 1
        return pltpu.make_async_remote_copy(
            src_ref=src,
            dst_ref=dst,
            send_sem=halo_send.at[int(up)],
            recv_sem=halo_recv.at[int(up)],
            device_id={"gx": to},
            device_id_type=MESH,
        )

    def feed(slot):
        return pltpu.make_async_remote_copy(
            src_ref=inflow,
            dst_ref=inlet.at[slot],
            send_sem=in_send,
            recv_sem=in_recv.at[slot],
            device_id={"gx": 0},
            device_id_type=MESH,
        )

    @pl.when(jnp.logical_not(has_high))
    def _():
        u[:, cx + 1] = jnp.zeros((3,) + u.shape[2:], jnp.float32)
        prov[0, cx + 1] = jnp.zeros(prov.shape[2:], jnp.float32)
        p1[cx + 4 : cx + 6] = jnp.zeros((2,) + p1.shape[1:], jnp.float32)
        part_in[1] = jnp.zeros(part_in.shape[1:], jnp.float32)

    @pl.when(jnp.logical_not(has_low))
    def _():
        prov[0, 0] = jnp.zeros(prov.shape[2:], jnp.float32)
        p1[0:2] = jnp.zeros((2,) + p1.shape[1:], jnp.float32)
        part_in[0] = jnp.zeros(part_in.shape[1:], jnp.float32)

    pl.semaphore_wait(barrier, n - 1)

    @pl.when(has_low)
    def _():
        feed(me).start()
        halo(False).start()

    @pl.when(has_high)
    def _():
        halo(True).start()

    zeros = jnp.zeros((16, rows.shape[1]), jnp.float32)
    rows[...] = zeros
    owners = 256 // SLOT
    wide = owners * cap
    source_lane = lax.broadcasted_iota(jnp.int32, (wide, 256), 0)
    slot_lane = lax.broadcasted_iota(jnp.int32, (wide, 256), 1)
    within = slot_lane & (SLOT - 1)
    picked = (source_lane == (slot_lane >> 4) * cap + within) & (within < cap)
    pick = jnp.where(picked, 1.0, 0.0)
    chunks = n // owners
    for copy in small:
        copy.wait()
    rows[0:3] = motion_in[...]
    rows[3:6] = axis_in[...]
    rows[6:7] = chord_in[...]
    rows[8:9] = (cell_in[...] + 1).astype(jnp.float32)
    rows[9:12] = frac_in[...]
    for q in range(chunks):
        spaced = lax.dot_general(
            rows[:, q * wide : (q + 1) * wide],
            pick,
            (((1,), (0,)), ((), ())),
            precision=lax.Precision.HIGHEST,
            preferred_element_type=jnp.float32,
        )
        table[q] = spaced[8:16]
        for h in range(256 // LANES):
            blocks[q * (256 // LANES) + h] = spaced[0:8, h * LANES : (h + 1) * LANES]

    per = LANES // SLOT

    def blade(k, to, slot):
        return pltpu.make_async_remote_copy(
            src_ref=blocks.at[to // per],
            dst_ref=arrived.at[slot],
            send_sem=blade_send.at[k],
            recv_sem=blade_recv.at[k],
            device_id={"gx": to},
            device_id_type=MESH,
        )

    def send_blade(k, carry):
        blade(k, lax.rem(me + k, n), me).start()
        return carry

    lax.fori_loop(1, n, send_blade, 0)
    arrived[me] = blocks[me // per]

    def wrap(ref, *lead):
        ref[(*lead, slice(PAD - 1, PAD))] = ref[(*lead, slice(PAD + ny - 1, PAD + ny))]
        ref[(*lead, slice(PAD + ny, PAD + ny + 1))] = ref[(*lead, slice(PAD, PAD + 1))]

    load.wait()
    for i in range(3):
        for x in range(cx):
            wrap(u, i, x + 1)

    depth_bits, span_bits = nz.bit_length() - 1, ny.bit_length() - 1
    layer = lax.broadcasted_iota(jnp.int32, (LANES, 256), 0)

    def weights(q):
        info = table[q]
        where = (info[0:1] + 0.5).astype(jnp.int32) - 1
        full = where >= 0
        a = where >> (depth_bits + span_bits)
        b = (where >> depth_bits) & (ny - 1)
        d = where & (nz - 1)
        fx, fy, fz = info[1:2], info[2:3], info[3:4]
        along_z = jnp.where(layer == d, 1.0 - fz, jnp.where(layer == d + 1, fz, 0.0))
        next_b = (b + 1) & (ny - 1)
        along_y = jnp.where(layer == b, 1.0 - fy, jnp.where(layer == next_b, fy, 0.0))
        along_x = []
        for x in range(cx):
            kept = jnp.where(a == x, 1.0 - fx, jnp.where(a + 1 == x, fx, 0.0))
            along_x.append(jnp.where(full, kept, 0.0))
        return along_x, along_y, split(along_z)

    sampled = []
    for q in range(chunks):
        along_x, along_y, along_z = weights(q)
        for i in range(3):
            total = jnp.zeros((1, 256), jnp.float32)
            for x in range(cx):
                lines = product(split(u[i, x + 1, body]), along_z, ((1,), (0,)))
                total = total + along_x[x] * jnp.sum(lines * along_y, axis=0, keepdims=True)
            sampled.append(total)

    first = lax.broadcasted_iota(jnp.int32, (ROWS, nz), 1) == 0
    last = lax.broadcasted_iota(jnp.int32, (ROWS, nz), 1) == nz - 1

    def deeper(value, edge=0.0):
        return jnp.where(last, edge, pltpu.roll(value, nz - 1, 1))

    def shallower(value, edge=0.0):
        return jnp.where(first, edge, pltpu.roll(value, 1, 1))

    starts = range(PAD, PAD + ny, ROWS)

    def at(start, shift=0):
        return pl.ds(start + shift, ROWS)

    def viscosity(p, low, mid, up):
        for s in starts:
            d = []
            for i in range(3):
                centre = u[i, mid, at(s)]
                d.append(
                    (
                        u[i, up, at(s)] - u[i, low, at(s)],
                        u[i, mid, at(s, 1)] - u[i, mid, at(s, -1)],
                        deeper(centre) - shallower(centre),
                    )
                )
            xy, xz, yz = d[0][1] + d[1][0], d[0][2] + d[2][0], d[1][2] + d[2][1]
            shear = d[0][0] * d[0][0] + d[1][1] * d[1][1] + d[2][2] * d[2][2]
            shear = shear + shear + (xy * xy + xz * xz + yz * yz) + 4.0 * STRAIN_FLOOR
            nu[p, at(s)] = (0.25 * TIME_STEP * SMAGORINSKY) * jnp.sqrt(shear)
        wrap(nu, p)

    def inner_viscosity(p, carry):
        viscosity(p + 1, p, p + 1, p + 2)
        return carry

    lax.fori_loop(1, cx - 1, inner_viscosity, 0)

    @pl.when(has_low)
    def _():
        halo(True).wait_recv()

    @pl.when(has_high)
    def _():
        halo(False).wait_recv()

    @pl.when(jnp.logical_not(has_low))
    def _():
        def take_inlet(k, carry):
            feed(k).wait_recv()
            return carry

        lax.fori_loop(1, n, take_inlet, 0)
        own = pltpu.make_async_copy(inflow, inlet.at[0], own_sem)
        own.start()
        own.wait()
        share = inflow.shape[1]
        for k in range(n):
            at = slice(PAD + k * share, PAD + (k + 1) * share)
            for i in range(3):
                u[i, 0, at] = inlet[k, i]

    for i in range(3):
        wrap(u, i, 0)
        wrap(u, i, cx + 1)

    def layer_of(up):
        return pltpu.make_async_remote_copy(
            src_ref=nu.at[cx if up else 1, body],
            dst_ref=nu.at[0 if up else cx + 1, body],
            send_sem=nu_send.at[int(up)],
            recv_sem=nu_recv.at[int(up)],
            device_id={"gx": me + 1 if up else me - 1},
            device_id_type=MESH,
        )

    viscosity(1, 0, 1, 2)

    @pl.when(has_low)
    def _():
        layer_of(False).start()

    viscosity(cx, cx - 1, cx, cx + 1)

    @pl.when(has_high)
    def _():
        layer_of(True).start()

    @pl.when(jnp.logical_not(has_low))
    def _():
        viscosity(0, 0, 0, 1)

    @pl.when(jnp.logical_not(has_high))
    def _():
        viscosity(cx + 1, cx, cx + 1, cx + 1)

    def take_blade(k, carry):
        blade(k, me, lax.rem(me + n - k, n)).wait_recv()
        return carry

    lax.fori_loop(1, n, take_blade, 0)
    lane = lax.broadcasted_iota(jnp.int32, (8, LANES), 1)
    mine = lax.rem(me, per)
    for q in range(chunks):
        halves = []
        for h in range(256 // LANES):
            block = jnp.zeros((8, LANES), jnp.float32)
            for o in range(per):
                shift = lax.rem(o - mine + per, per) * SLOT
                moved = pltpu.roll(arrived[(q * (256 // LANES) + h) * per + o], shift, 1)
                block = jnp.where((lane >> 4) == o, moved, block)
            halves.append(block)
        point = jnp.concatenate(halves, axis=1)
        along_x, along_y, along_z = weights(q)
        r = [sampled[3 * q + i] - point[i : i + 1] for i in range(3)]
        e = [point[3 + i : 4 + i] for i in range(3)]
        speed = jnp.sqrt(r[0] * r[0] + r[1] * r[1] + r[2] * r[2] + STRAIN_FLOOR)
        size = (TIME_STEP * FORCE_SCALE) * point[6:7] * speed
        lift = [
            r[1] * e[2] - r[2] * e[1],
            r[2] * e[0] - r[0] * e[2],
            r[0] * e[1] - r[1] * e[0],
        ]
        for i in range(3):
            force = size * (lift[i] - r[i])
            for x in range(cx):
                laid = product(
                    split(along_y * (force * along_x[x])), along_z, ((1,), (1,))
                )
                if q == 0:
                    prov[i, x + 1, body] = laid
                else:
                    prov[i, x + 1, body] += laid

    def momentum(p):
        for s in starts:
            centre = [u[i, p + 1, at(s)] for i in range(3)]
            own = nu[p + 1, at(s)]
            edge = centre[2] * centre[2]
            edge = edge + edge + centre[0] * centre[0] + centre[1] * centre[1]
            edge = (0.25 * TIME_STEP * SMAGORINSKY) * jnp.sqrt(edge + 4.0 * STRAIN_FLOOR)
            carried = [(0.5 * TIME_STEP) * value for value in centre]
            coef = [
                own + nu[p + 2, at(s)] - carried[0],
                own + nu[p, at(s)] + carried[0],
                own + nu[p + 1, at(s, 1)] - carried[1],
                own + nu[p + 1, at(s, -1)] + carried[1],
                own + deeper(own, edge) - carried[2],
                own + shallower(own, edge) + carried[2],
            ]
            rest = 1.0 - (coef[0] + coef[1] + coef[2] + coef[3] + coef[4] + coef[5])
            for i in range(3):
                value = prov[i, p + 1, at(s)] + rest * centre[i]
                value = value + coef[0] * u[i, p + 2, at(s)] + coef[1] * u[i, p, at(s)]
                value = value + coef[2] * u[i, p + 1, at(s, 1)] + coef[3] * u[i, p + 1, at(s, -1)]
                value = value + coef[4] * deeper(centre[i]) + coef[5] * shallower(centre[i])
                prov[i, p + 1, at(s)] = value
        wrap(prov, 1, p + 1)

    def inner_momentum(p, carry):
        momentum(p)
        return carry

    lax.fori_loop(1, cx - 1, inner_momentum, 0)

    scale = -1.0 / 12.0

    def flat_part(p, s):
        w = prov[2, p + 1, at(s)]
        return prov[1, p + 1, at(s, 1)] - prov[1, p + 1, at(s, -1)] + deeper(w) - shallower(w)

    def rim(up, what):
        if what == 0:
            src = prov.at[0, cx if up else 1, body]
            dst = prov.at[0, 0 if up else cx + 1, body]
        elif what == 1:
            src = part_out.at[1 if up else 0]
            dst = part_in.at[0 if up else 1]
        else:
            plane = cx - 5 + what if up else what - 1
            src = p1.at[plane + 3, body]
            dst = p1.at[plane + 3 - cx if up else plane + 3 + cx, body]
        k = 4 * int(up) + what
        return pltpu.make_async_remote_copy(
            src_ref=src,
            dst_ref=dst,
            send_sem=rim_send.at[k],
            recv_sem=rim_recv.at[k],
            device_id={"gx": me + 1 if up else me - 1},
            device_id_type=MESH,
        )

    def send_rim(up, what):
        @pl.when(has_high if up else has_low)
        def _():
            rim(up, what).start()

    def first_potential(p):
        for s in starts:
            p1[p + 3, at(s)] = scale * (
                flat_part(p, s) + prov[0, p + 2, at(s)] - prov[0, p, at(s)]
            )

    @pl.when(has_low)
    def _():
        layer_of(True).wait_recv()

    momentum(0)
    send_rim(False, 0)
    for s in starts:
        part_out[0, pl.ds(s - PAD, ROWS)] = scale * (flat_part(0, s) + prov[0, 2, at(s)])
    send_rim(False, 1)
    for p in range(1, cx - 2):
        first_potential(p)
    send_rim(False, 2)
    send_rim(True, 2)

    @pl.when(has_high)
    def _():
        layer_of(False).wait_recv()

    momentum(cx - 1)
    send_rim(True, 0)
    for s in starts:
        part_out[1, pl.ds(s - PAD, ROWS)] = scale * (
            flat_part(cx - 1, s) - prov[0, cx - 1, at(s)]
        )
    send_rim(True, 1)
    first_potential(cx - 2)
    send_rim(False, 3)
    send_rim(True, 3)
    keep = pltpu.make_async_copy(prov.at[:, 1 : 1 + cx, body], given, keep_sem)
    keep.start()
    for p in range(1, cx - 1):
        wrap(p1, p + 3)

    for what in range(4):

        @pl.when(has_low)
        def _():
            rim(True, what).wait_recv()

        @pl.when(has_high)
        def _():
            rim(False, what).wait_recv()

    for s in starts:
        o = pl.ds(s - PAD, ROWS)
        p1[3, at(s)] = part_out[0, o] - scale * prov[0, 0, at(s)]
        p1[cx + 2, at(s)] = part_out[1, o] + scale * prov[0, cx + 1, at(s)]
        p1[2, at(s)] = low_ok * (part_in[0, o] + scale * prov[0, 1, at(s)])
        p1[cx + 3, at(s)] = high_ok * (part_in[1, o] - scale * prov[0, cx, at(s)])
    for p in (1, 2, 3, cx + 2, cx + 3, cx + 4):
        wrap(p1, p)

    def sweep(old, new, back):
        planes = new.shape[0]
        outer = (planes - cx) // 2

        def plane(p, carry):
            ok = jnp.where(p < outer, low_ok, jnp.where(p >= outer + cx, high_ok, 1.0))
            for s in starts:
                centre = old[p + 1, at(s)]
                near = old[p, at(s)] + old[p + 2, at(s)]
                near = near + old[p + 1, at(s, 1)] + old[p + 1, at(s, -1)]
                near = near + deeper(centre) + shallower(centre)
                new[p, at(s)] = ok * (near * (1.0 / 6.0) + p1[p + back, at(s)])
            wrap(new, p)
            return carry

        lax.fori_loop(0, planes, plane, 0)

    sweep(p1, p2, 1)
    sweep(p2, p3, 2)

    def store(p):
        return pltpu.make_async_copy(result.at[:, p], change.at[:, p], store_sem.at[p])

    def correct(p, carry):
        for s in starts:
            o = pl.ds(s - PAD, ROWS)
            centre = p3[p + 1, at(s)]
            result[0, p, o] = 0.5 * (p3[p + 2, at(s)] - p3[p, at(s)])
            result[1, p, o] = 0.5 * (p3[p + 1, at(s, 1)] - p3[p + 1, at(s, -1)])
            result[2, p, o] = 0.5 * (deeper(centre) - shallower(centre))
        store(p).start()
        return carry

    lax.fori_loop(0, cx, correct, 0)

    def sent_blade(k, carry):
        blade(k, lax.rem(me + k, n), me).wait_send()
        return carry

    lax.fori_loop(1, n, sent_blade, 0)
    keep.wait()
    for p in range(cx):
        store(p).wait()

    @pl.when(has_low)
    def _():
        feed(me).wait_send()
        halo(False).wait_send()
        layer_of(False).wait_send()
        for what in range(4):
            rim(False, what).wait_send()

    @pl.when(has_high)
    def _():
        halo(True).wait_send()
        layer_of(True).wait_send()
        for what in range(4):
            rim(True, what).wait_send()


def shards(n, velocity, inflow, blade_motion, blade_axis, blade_chord, host_cell, host_frac):
    cx, ny, nz = velocity.shape[1:]
    slots = host_cell.shape[0]
    high = PAD + ny + 8
    vmem = pltpu.VMEM
    f32 = jnp.float32
    dma = pltpu.SemaphoreType.DMA
    provisional, gradient = pl.pallas_call(
        functools.partial(kernel, n),
        out_shape=[jax.ShapeDtypeStruct(velocity.shape, f32)] * 2,
        in_specs=[pl.BlockSpec(memory_space=pltpu.HBM)] * 7,
        out_specs=[pl.BlockSpec(memory_space=pltpu.HBM)] * 2,
        scratch_shapes=[
            vmem((3, slots), f32),
            vmem((3, slots), f32),
            vmem((1, slots), f32),
            vmem((1, slots), jnp.int32),
            vmem((3, slots), f32),
            vmem((3, cx + 2, high, nz), f32),
            vmem((cx + 2, high, nz), f32),
            vmem((3, cx + 2, high, nz), f32),
            vmem((cx + 6, high, nz), f32),
            vmem((cx + 4, high, nz), f32),
            vmem((cx + 2, high, nz), f32),
            vmem((2, ny, nz), f32),
            vmem((2, ny, nz), f32),
            vmem((16, slots), f32),
            vmem((n * SLOT // LANES, 8, LANES), f32),
            vmem((n * SLOT // 256, 8, 256), f32),
            vmem((n, 8, LANES), f32),
            vmem((n,) + inflow.shape, f32),
            dma,
            dma((5,)),
            dma,
            dma((2,)),
            dma((2,)),
            dma((n,)),
            dma((n,)),
            dma,
            dma((n,)),
            dma((2,)),
            dma((2,)),
            dma((8,)),
            dma((8,)),
            vmem(velocity.shape, f32),
            dma,
            dma((cx,)),
        ],
        compiler_params=pltpu.CompilerParams(
            collective_id=0, has_side_effects=True, vmem_limit_bytes=64 * 1024 * 1024 - 65536
        ),
    )(
        velocity,
        inflow,
        blade_motion,
        blade_axis,
        blade_chord.reshape(1, slots),
        host_cell.reshape(1, slots),
        host_frac,
    )
    return provisional - gradient


def solution(mesh):
    return jax.shard_map(
        functools.partial(shards, mesh.shape["gx"]),
        mesh=mesh,
        in_specs=(
            P("runs", "gx", None, None),
            P("runs", "gx", None),
            P("runs", "gx"),
            P("runs", "gx"),
            P(("runs", "gx")),
            P(("runs", "gx")),
            P("runs", "gx"),
        ),
        out_specs=P("runs", "gx", None, None),
        check_vma=False,
    )
```

```python
import functools

import jax
import jax.numpy as jnp
from jax import lax
from jax.experimental import pallas as pl
from jax.experimental.pallas import tpu as pltpu
from jax.sharding import PartitionSpec as P

TIME_STEP = 0.2
SMAGORINSKY = 0.0289
STRAIN_FLOOR = 0.01
FORCE_SCALE = 0.2

MESH = pl.DeviceIdType.MESH
PAD = 8
ROWS = 16
SLOT = 16
LANES = 128


def split(value):
    high = value.astype(jnp.bfloat16)
    return high, (value - high.astype(jnp.float32)).astype(jnp.bfloat16)


def product(left, right, contract):
    def one(a, b):
        return lax.dot_general(
            a, b, (contract, ((), ())), preferred_element_type=jnp.float32
        )

    return one(left[0], right[0]) + (one(left[0], right[1]) + one(left[1], right[0]))


def kernel(
    n,
    vel,
    inflow,
    motion,
    axis,
    chord,
    cell,
    frac,
    given,
    potential,
    motion_in,
    axis_in,
    chord_in,
    cell_in,
    frac_in,
    u,
    nu,
    prov,
    p1,
    p2,
    p3,
    part_out,
    part_in,
    rows,
    blocks,
    table,
    arrived,
    inlet,
    load_sem,
    small_sem,
    own_sem,
    halo_send,
    halo_recv,
    blade_send,
    blade_recv,
    in_send,
    in_recv,
    nu_send,
    nu_recv,
    rim_send,
    rim_recv,
    keep_sem,
    store_sem,
):
    me = lax.axis_index("gx")
    cx, ny, nz = vel.shape[1:]
    cap = cell.shape[1] // n
    body = pl.ds(PAD, ny)
    has_low, has_high = me > 0, me < n - 1
    low_ok = jnp.where(has_low, 1.0, 0.0)
    high_ok = jnp.where(has_high, 1.0, 0.0)

    barrier = pltpu.get_barrier_semaphore()

    def greet(k, carry):
        pl.semaphore_signal(
            barrier, inc=1, device_id={"gx": lax.rem(me + k, n)}, device_id_type=MESH
        )
        return carry

    lax.fori_loop(1, n, greet, 0)
    pairs = (
        (motion, motion_in),
        (axis, axis_in),
        (chord, chord_in),
        (cell, cell_in),
        (frac, frac_in),
    )
    small = [pltpu.make_async_copy(a, b, small_sem.at[k]) for k, (a, b) in enumerate(pairs)]
    for copy in small:
        copy.start()
    load = pltpu.make_async_copy(vel, u.at[:, 1 : 1 + cx, body], load_sem)
    load.start()

    def halo(up):
        if up:
            src, dst, to = vel.at[:, cx - 1], u.at[:, 0, body], me + 1
        else:
            src, dst, to = vel.at[:, 0], u.at[:, cx + 1, body], me - 1
        return pltpu.make_async_remote_copy(
            src_ref=src,
            dst_ref=dst,
            send_sem=halo_send.at[int(up)],
            recv_sem=halo_recv.at[int(up)],
            device_id={"gx": to},
            device_id_type=MESH,
        )

    def feed(slot):
        return pltpu.make_async_remote_copy(
            src_ref=inflow,
            dst_ref=inlet.at[slot],
            send_sem=in_send,
            recv_sem=in_recv.at[slot],
            device_id={"gx": 0},
            device_id_type=MESH,
        )

    @pl.when(jnp.logical_not(has_high))
    def _():
        u[:, cx + 1] = jnp.zeros((3,) + u.shape[2:], jnp.float32)
        prov[0, cx + 1] = jnp.zeros(prov.shape[2:], jnp.float32)
        p1[cx + 4 : cx + 6] = jnp.zeros((2,) + p1.shape[1:], jnp.float32)
        part_in[1] = jnp.zeros(part_in.shape[1:], jnp.float32)

    @pl.when(jnp.logical_not(has_low))
    def _():
        prov[0, 0] = jnp.zeros(prov.shape[2:], jnp.float32)
        p1[0:2] = jnp.zeros((2,) + p1.shape[1:], jnp.float32)
        part_in[0] = jnp.zeros(part_in.shape[1:], jnp.float32)

    pl.semaphore_wait(barrier, n - 1)

    @pl.when(has_low)
    def _():
        feed(me).start()
        halo(False).start()

    @pl.when(has_high)
    def _():
        halo(True).start()

    zeros = jnp.zeros((16, rows.shape[1]), jnp.float32)
    rows[...] = zeros
    owners = 256 // SLOT
    wide = owners * cap
    source_lane = lax.broadcasted_iota(jnp.int32, (wide, 256), 0)
    slot_lane = lax.broadcasted_iota(jnp.int32, (wide, 256), 1)
    within = slot_lane & (SLOT - 1)
    picked = (source_lane == (slot_lane >> 4) * cap + within) & (within < cap)
    pick = jnp.where(picked, 1.0, 0.0)
    chunks = n // owners
    for copy in small:
        copy.wait()
    rows[0:3] = motion_in[...]
    rows[3:6] = axis_in[...]
    rows[6:7] = chord_in[...]
    rows[8:9] = (cell_in[...] + 1).astype(jnp.float32)
    rows[9:12] = frac_in[...]
    for q in range(chunks):
        spaced = lax.dot_general(
            rows[:, q * wide : (q + 1) * wide],
            pick,
            (((1,), (0,)), ((), ())),
            precision=lax.Precision.HIGHEST,
            preferred_element_type=jnp.float32,
        )
        table[q] = spaced[8:16]
        for h in range(256 // LANES):
            blocks[q * (256 // LANES) + h] = spaced[0:8, h * LANES : (h + 1) * LANES]

    per = LANES // SLOT

    def blade(k, to, slot):
        return pltpu.make_async_remote_copy(
            src_ref=blocks.at[to // per],
            dst_ref=arrived.at[slot],
            send_sem=blade_send.at[k],
            recv_sem=blade_recv.at[k],
            device_id={"gx": to},
            device_id_type=MESH,
        )

    def send_blade(k, carry):
        blade(k, lax.rem(me + k, n), me).start()
        return carry

    lax.fori_loop(1, n, send_blade, 0)
    arrived[me] = blocks[me // per]

    def wrap(ref, *lead):
        ref[(*lead, slice(PAD - 1, PAD))] = ref[(*lead, slice(PAD + ny - 1, PAD + ny))]
        ref[(*lead, slice(PAD + ny, PAD + ny + 1))] = ref[(*lead, slice(PAD, PAD + 1))]

    load.wait()
    for i in range(3):
        for x in range(cx):
            wrap(u, i, x + 1)

    depth_bits, span_bits = nz.bit_length() - 1, ny.bit_length() - 1
    layer = lax.broadcasted_iota(jnp.int32, (LANES, 256), 0)

    def weights(q):
        info = table[q]
        where = (info[0:1] + 0.5).astype(jnp.int32) - 1
        full = where >= 0
        a = where >> (depth_bits + span_bits)
        b = (where >> depth_bits) & (ny - 1)
        d = where & (nz - 1)
        fx, fy, fz = info[1:2], info[2:3], info[3:4]
        along_z = jnp.where(layer == d, 1.0 - fz, jnp.where(layer == d + 1, fz, 0.0))
        next_b = (b + 1) & (ny - 1)
        along_y = jnp.where(layer == b, 1.0 - fy, jnp.where(layer == next_b, fy, 0.0))
        along_x = []
        for x in range(cx):
            kept = jnp.where(a == x, 1.0 - fx, jnp.where(a + 1 == x, fx, 0.0))
            along_x.append(jnp.where(full, kept, 0.0))
        return along_x, along_y, split(along_z)

    sampled = []
    for q in range(chunks):
        along_x, along_y, along_z = weights(q)
        for i in range(3):
            total = jnp.zeros((1, 256), jnp.float32)
            for x in range(cx):
                lines = product(split(u[i, x + 1, body]), along_z, ((1,), (0,)))
                total = total + along_x[x] * jnp.sum(lines * along_y, axis=0, keepdims=True)
            sampled.append(total)

    first = lax.broadcasted_iota(jnp.int32, (ROWS, nz), 1) == 0
    last = lax.broadcasted_iota(jnp.int32, (ROWS, nz), 1) == nz - 1

    def deeper(value, edge=0.0):
        return jnp.where(last, edge, pltpu.roll(value, nz - 1, 1))

    def shallower(value, edge=0.0):
        return jnp.where(first, edge, pltpu.roll(value, 1, 1))

    starts = range(PAD, PAD + ny, ROWS)

    def at(start, shift=0):
        return pl.ds(start + shift, ROWS)

    def viscosity(p, low, mid, up):
        for s in starts:
            d = []
            for i in range(3):
                centre = u[i, mid, at(s)]
                d.append(
                    (
                        u[i, up, at(s)] - u[i, low, at(s)],
                        u[i, mid, at(s, 1)] - u[i, mid, at(s, -1)],
                        deeper(centre) - shallower(centre),
                    )
                )
            xy, xz, yz = d[0][1] + d[1][0], d[0][2] + d[2][0], d[1][2] + d[2][1]
            shear = d[0][0] * d[0][0] + d[1][1] * d[1][1] + d[2][2] * d[2][2]
            shear = shear + shear + (xy * xy + xz * xz + yz * yz) + 4.0 * STRAIN_FLOOR
            nu[p, at(s)] = (0.25 * TIME_STEP * SMAGORINSKY) * jnp.sqrt(shear)
        wrap(nu, p)

    def inner_viscosity(p, carry):
        viscosity(p + 1, p, p + 1, p + 2)
        return carry

    lax.fori_loop(1, cx - 1, inner_viscosity, 0)

    @pl.when(has_low)
    def _():
        halo(True).wait_recv()

    @pl.when(has_high)
    def _():
        halo(False).wait_recv()

    @pl.when(jnp.logical_not(has_low))
    def _():
        def take_inlet(k, carry):
            feed(k).wait_recv()
            return carry

        lax.fori_loop(1, n, take_inlet, 0)
        own = pltpu.make_async_copy(inflow, inlet.at[0], own_sem)
        own.start()
        own.wait()
        share = inflow.shape[1]
        for k in range(n):
            at = slice(PAD + k * share, PAD + (k + 1) * share)
            for i in range(3):
                u[i, 0, at] = inlet[k, i]

    for i in range(3):
        wrap(u, i, 0)
        wrap(u, i, cx + 1)

    def layer_of(up):
        return pltpu.make_async_remote_copy(
            src_ref=nu.at[cx if up else 1, body],
            dst_ref=nu.at[0 if up else cx + 1, body],
            send_sem=nu_send.at[int(up)],
            recv_sem=nu_recv.at[int(up)],
            device_id={"gx": me + 1 if up else me - 1},
            device_id_type=MESH,
        )

    viscosity(1, 0, 1, 2)

    @pl.when(has_low)
    def _():
        layer_of(False).start()

    viscosity(cx, cx - 1, cx, cx + 1)

    @pl.when(has_high)
    def _():
        layer_of(True).start()

    @pl.when(jnp.logical_not(has_low))
    def _():
        viscosity(0, 0, 0, 1)

    @pl.when(jnp.logical_not(has_high))
    def _():
        viscosity(cx + 1, cx, cx + 1, cx + 1)

    def take_blade(k, carry):
        blade(k, me, lax.rem(me + n - k, n)).wait_recv()
        return carry

    lax.fori_loop(1, n, take_blade, 0)
    lane = lax.broadcasted_iota(jnp.int32, (8, LANES), 1)
    mine = lax.rem(me, per)
    for q in range(chunks):
        halves = []
        for h in range(256 // LANES):
            block = jnp.zeros((8, LANES), jnp.float32)
            for o in range(per):
                shift = lax.rem(o - mine + per, per) * SLOT
                moved = pltpu.roll(arrived[(q * (256 // LANES) + h) * per + o], shift, 1)
                block = jnp.where((lane >> 4) == o, moved, block)
            halves.append(block)
        point = jnp.concatenate(halves, axis=1)
        along_x, along_y, along_z = weights(q)
        r = [sampled[3 * q + i] - point[i : i + 1] for i in range(3)]
        e = [point[3 + i : 4 + i] for i in range(3)]
        speed = jnp.sqrt(r[0] * r[0] + r[1] * r[1] + r[2] * r[2] + STRAIN_FLOOR)
        size = (TIME_STEP * FORCE_SCALE) * point[6:7] * speed
        lift = [
            r[1] * e[2] - r[2] * e[1],
            r[2] * e[0] - r[0] * e[2],
            r[0] * e[1] - r[1] * e[0],
        ]
        for i in range(3):
            force = size * (lift[i] - r[i])
            for x in range(cx):
                laid = product(
                    split(along_y * (force * along_x[x])), along_z, ((1,), (1,))
                )
                if q == 0:
                    prov[i, x + 1, body] = laid
                else:
                    prov[i, x + 1, body] += laid

    def momentum(p):
        for s in starts:
            centre = [u[i, p + 1, at(s)] for i in range(3)]
            own = nu[p + 1, at(s)]
            edge = centre[2] * centre[2]
            edge = edge + edge + centre[0] * centre[0] + centre[1] * centre[1]
            edge = (0.25 * TIME_STEP * SMAGORINSKY) * jnp.sqrt(edge + 4.0 * STRAIN_FLOOR)
            carried = [(0.5 * TIME_STEP) * value for value in centre]
            coef = [
                own + nu[p + 2, at(s)] - carried[0],
                own + nu[p, at(s)] + carried[0],
                own + nu[p + 1, at(s, 1)] - carried[1],
                own + nu[p + 1, at(s, -1)] + carried[1],
                own + deeper(own, edge) - carried[2],
                own + shallower(own, edge) + carried[2],
            ]
            rest = 1.0 - (coef[0] + coef[1] + coef[2] + coef[3] + coef[4] + coef[5])
            for i in range(3):
                value = prov[i, p + 1, at(s)] + rest * centre[i]
                value = value + coef[0] * u[i, p + 2, at(s)] + coef[1] * u[i, p, at(s)]
                value = value + coef[2] * u[i, p + 1, at(s, 1)] + coef[3] * u[i, p + 1, at(s, -1)]
                value = value + coef[4] * deeper(centre[i]) + coef[5] * shallower(centre[i])
                prov[i, p + 1, at(s)] = value
        wrap(prov, 1, p + 1)

    def inner_momentum(p, carry):
        momentum(p)
        return carry

    lax.fori_loop(1, cx - 1, inner_momentum, 0)

    scale = -1.0 / 12.0

    def flat_part(p, s):
        w = prov[2, p + 1, at(s)]
        return prov[1, p + 1, at(s, 1)] - prov[1, p + 1, at(s, -1)] + deeper(w) - shallower(w)

    def rim(up, what):
        if what == 0:
            src = prov.at[0, cx if up else 1, body]
            dst = prov.at[0, 0 if up else cx + 1, body]
        elif what == 1:
            src = part_out.at[1 if up else 0]
            dst = part_in.at[0 if up else 1]
        else:
            plane = cx - 5 + what if up else what - 1
            src = p1.at[plane + 3, body]
            dst = p1.at[plane + 3 - cx if up else plane + 3 + cx, body]
        k = 4 * int(up) + what
        return pltpu.make_async_remote_copy(
            src_ref=src,
            dst_ref=dst,
            send_sem=rim_send.at[k],
            recv_sem=rim_recv.at[k],
            device_id={"gx": me + 1 if up else me - 1},
            device_id_type=MESH,
        )

    def send_rim(up, what):
        @pl.when(has_high if up else has_low)
        def _():
            rim(up, what).start()

    def first_potential(p):
        for s in starts:
            p1[p + 3, at(s)] = scale * (
                flat_part(p, s) + prov[0, p + 2, at(s)] - prov[0, p, at(s)]
            )

    @pl.when(has_low)
    def _():
        layer_of(True).wait_recv()

    momentum(0)
    send_rim(False, 0)
    for s in starts:
        part_out[0, pl.ds(s - PAD, ROWS)] = scale * (flat_part(0, s) + prov[0, 2, at(s)])
    send_rim(False, 1)
    for p in range(1, cx - 2):
        first_potential(p)
    send_rim(False, 2)
    send_rim(True, 2)

    @pl.when(has_high)
    def _():
        layer_of(False).wait_recv()

    momentum(cx - 1)
    send_rim(True, 0)
    for s in starts:
        part_out[1, pl.ds(s - PAD, ROWS)] = scale * (
            flat_part(cx - 1, s) - prov[0, cx - 1, at(s)]
        )
    send_rim(True, 1)
    first_potential(cx - 2)
    send_rim(False, 3)
    send_rim(True, 3)
    keep = pltpu.make_async_copy(prov.at[:, 1 : 1 + cx, body], given, keep_sem)
    keep.start()
    for p in range(1, cx - 1):
        wrap(p1, p + 3)

    for what in range(4):

        @pl.when(has_low)
        def _():
            rim(True, what).wait_recv()

        @pl.when(has_high)
        def _():
            rim(False, what).wait_recv()

    for s in starts:
        o = pl.ds(s - PAD, ROWS)
        p1[3, at(s)] = part_out[0, o] - scale * prov[0, 0, at(s)]
        p1[cx + 2, at(s)] = part_out[1, o] + scale * prov[0, cx + 1, at(s)]
        p1[2, at(s)] = low_ok * (part_in[0, o] + scale * prov[0, 1, at(s)])
        p1[cx + 3, at(s)] = high_ok * (part_in[1, o] - scale * prov[0, cx, at(s)])
    for p in (1, 2, 3, cx + 2, cx + 3, cx + 4):
        wrap(p1, p)

    def store(p):
        return pltpu.make_async_copy(p3.at[p], potential.at[p], store_sem.at[p])

    def sweep(old, new, back, done=None):
        planes = new.shape[0]
        outer = (planes - cx) // 2

        def plane(p, carry):
            ok = jnp.where(p < outer, low_ok, jnp.where(p >= outer + cx, high_ok, 1.0))
            for s in starts:
                centre = old[p + 1, at(s)]
                near = old[p, at(s)] + old[p + 2, at(s)]
                near = near + old[p + 1, at(s, 1)] + old[p + 1, at(s, -1)]
                near = near + deeper(centre) + shallower(centre)
                new[p, at(s)] = ok * (near * (1.0 / 6.0) + p1[p + back, at(s)])
            wrap(new, p)
            if done is not None:
                done(p)
            return carry

        lax.fori_loop(0, planes, plane, 0)

    sweep(p1, p2, 1)
    sweep(p2, p3, 2, lambda p: store(p).start())

    def sent_blade(k, carry):
        blade(k, lax.rem(me + k, n), me).wait_send()
        return carry

    lax.fori_loop(1, n, sent_blade, 0)
    keep.wait()
    for p in range(cx + 2):
        store(p).wait()

    @pl.when(has_low)
    def _():
        feed(me).wait_send()
        halo(False).wait_send()
        layer_of(False).wait_send()
        for what in range(4):
            rim(False, what).wait_send()

    @pl.when(has_high)
    def _():
        halo(True).wait_send()
        layer_of(True).wait_send()
        for what in range(4):
            rim(True, what).wait_send()


def correct(given, below, here, above, out):
    ny, nz = given.shape[2:]
    spot = lax.broadcasted_iota(jnp.int32, (ROWS, nz), 1)
    for s in range(0, ny, ROWS):
        o = pl.ds(s, ROWS)
        row = pl.ds(PAD + s, ROWS)
        centre = here[0, row]
        deeper = jnp.where(spot == nz - 1, 0.0, pltpu.roll(centre, nz - 1, 1))
        shallower = jnp.where(spot == 0, 0.0, pltpu.roll(centre, 1, 1))
        along_y = here[0, pl.ds(PAD + s + 1, ROWS)] - here[0, pl.ds(PAD + s - 1, ROWS)]
        out[0, 0, o] = given[0, 0, o] - 0.5 * (above[0, row] - below[0, row])
        out[1, 0, o] = given[1, 0, o] - 0.5 * along_y
        out[2, 0, o] = given[2, 0, o] - 0.5 * (deeper - shallower)


def shards(n, velocity, inflow, blade_motion, blade_axis, blade_chord, host_cell, host_frac):
    cx, ny, nz = velocity.shape[1:]
    slots = host_cell.shape[0]
    high = PAD + ny + 8
    vmem = pltpu.VMEM
    f32 = jnp.float32
    dma = pltpu.SemaphoreType.DMA
    provisional, potential = pl.pallas_call(
        functools.partial(kernel, n),
        out_shape=[
            jax.ShapeDtypeStruct(velocity.shape, f32),
            jax.ShapeDtypeStruct((cx + 2, high, nz), f32),
        ],
        in_specs=[pl.BlockSpec(memory_space=pltpu.HBM)] * 7,
        out_specs=[pl.BlockSpec(memory_space=pltpu.HBM)] * 2,
        scratch_shapes=[
            vmem((3, slots), f32),
            vmem((3, slots), f32),
            vmem((1, slots), f32),
            vmem((1, slots), jnp.int32),
            vmem((3, slots), f32),
            vmem((3, cx + 2, high, nz), f32),
            vmem((cx + 2, high, nz), f32),
            vmem((3, cx + 2, high, nz), f32),
            vmem((cx + 6, high, nz), f32),
            vmem((cx + 4, high, nz), f32),
            vmem((cx + 2, high, nz), f32),
            vmem((2, ny, nz), f32),
            vmem((2, ny, nz), f32),
            vmem((16, slots), f32),
            vmem((n * SLOT // LANES, 8, LANES), f32),
            vmem((n * SLOT // 256, 8, 256), f32),
            vmem((n, 8, LANES), f32),
            vmem((n,) + inflow.shape, f32),
            dma,
            dma((5,)),
            dma,
            dma((2,)),
            dma((2,)),
            dma((n,)),
            dma((n,)),
            dma,
            dma((n,)),
            dma((2,)),
            dma((2,)),
            dma((8,)),
            dma((8,)),
            dma,
            dma((cx + 2,)),
        ],
        compiler_params=pltpu.CompilerParams(
            collective_id=0, has_side_effects=True, vmem_limit_bytes=64 * 1024 * 1024 - 65536
        ),
    )(
        velocity,
        inflow,
        blade_motion,
        blade_axis,
        blade_chord.reshape(1, slots),
        host_cell.reshape(1, slots),
        host_frac,
    )
    block = pl.BlockSpec((3, 1, ny, nz), lambda p: (0, p, 0, 0))
    near = [pl.BlockSpec((1, high, nz), lambda p, k=k: (p + k, 0, 0)) for k in range(3)]
    return pl.pallas_call(
        correct,
        out_shape=jax.ShapeDtypeStruct(velocity.shape, f32),
        grid=(cx,),
        in_specs=[block] + near,
        out_specs=block,
        compiler_params=pltpu.CompilerParams(vmem_limit_bytes=64 * 1024 * 1024 - 65536),
    )(provisional, potential, potential, potential)


def solution(mesh):
    return jax.shard_map(
        functools.partial(shards, mesh.shape["gx"]),
        mesh=mesh,
        in_specs=(
            P("runs", "gx", None, None),
            P("runs", "gx", None),
            P("runs", "gx"),
            P("runs", "gx"),
            P(("runs", "gx")),
            P(("runs", "gx")),
            P("runs", "gx"),
        ),
        out_specs=P("runs", "gx", None, None),
        check_vma=False,
    )
```

```python
import functools

import jax
import jax.numpy as jnp
from jax import lax
from jax.experimental import pallas as pl
from jax.experimental.pallas import tpu as pltpu
from jax.sharding import PartitionSpec as P

TIME_STEP = 0.2
SMAGORINSKY = 0.0289
STRAIN_FLOOR = 0.01
FORCE_SCALE = 0.2

MESH = pl.DeviceIdType.MESH
PAD = 8
ROWS = 16
SLOT = 16
LANES = 128


def split(value):
    high = value.astype(jnp.bfloat16)
    return high, (value - high.astype(jnp.float32)).astype(jnp.bfloat16)


def product(left, right, contract):
    def one(a, b):
        return lax.dot_general(
            a, b, (contract, ((), ())), preferred_element_type=jnp.float32
        )

    return one(left[0], right[0]) + (one(left[0], right[1]) + one(left[1], right[0]))


def kernel(
    n,
    vel,
    inflow,
    motion,
    axis,
    chord,
    cell,
    frac,
    change,
    motion_in,
    axis_in,
    chord_in,
    cell_in,
    frac_in,
    u,
    nu,
    prov,
    p1,
    p2,
    p3,
    part_out,
    part_in,
    rows,
    blocks,
    table,
    arrived,
    inlet,
    load_sem,
    small_sem,
    own_sem,
    halo_send,
    halo_recv,
    blade_send,
    blade_recv,
    in_send,
    in_recv,
    nu_send,
    nu_recv,
    rim_send,
    rim_recv,
    result,
    store_sem,
):
    me = lax.axis_index("gx")
    cx, ny, nz = vel.shape[1:]
    cap = cell.shape[1] // n
    body = pl.ds(PAD, ny)
    has_low, has_high = me > 0, me < n - 1
    low_ok = jnp.where(has_low, 1.0, 0.0)
    high_ok = jnp.where(has_high, 1.0, 0.0)

    barrier = pltpu.get_barrier_semaphore()

    def greet(k, carry):
        pl.semaphore_signal(
            barrier, inc=1, device_id={"gx": lax.rem(me + k, n)}, device_id_type=MESH
        )
        return carry

    lax.fori_loop(1, n, greet, 0)
    pairs = (
        (motion, motion_in),
        (axis, axis_in),
        (chord, chord_in),
        (cell, cell_in),
        (frac, frac_in),
    )
    small = [pltpu.make_async_copy(a, b, small_sem.at[k]) for k, (a, b) in enumerate(pairs)]
    for copy in small:
        copy.start()
    load = pltpu.make_async_copy(vel, u.at[:, 1 : 1 + cx, body], load_sem)
    load.start()

    def halo(up):
        if up:
            src, dst, to = vel.at[:, cx - 1], u.at[:, 0, body], me + 1
        else:
            src, dst, to = vel.at[:, 0], u.at[:, cx + 1, body], me - 1
        return pltpu.make_async_remote_copy(
            src_ref=src,
            dst_ref=dst,
            send_sem=halo_send.at[int(up)],
            recv_sem=halo_recv.at[int(up)],
            device_id={"gx": to},
            device_id_type=MESH,
        )

    def feed(slot):
        return pltpu.make_async_remote_copy(
            src_ref=inflow,
            dst_ref=inlet.at[slot],
            send_sem=in_send,
            recv_sem=in_recv.at[slot],
            device_id={"gx": 0},
            device_id_type=MESH,
        )

    @pl.when(jnp.logical_not(has_high))
    def _():
        u[:, cx + 1] = jnp.zeros((3,) + u.shape[2:], jnp.float32)
        prov[0, cx + 1] = jnp.zeros(prov.shape[2:], jnp.float32)
        p1[cx + 4 : cx + 6] = jnp.zeros((2,) + p1.shape[1:], jnp.float32)
        part_in[1] = jnp.zeros(part_in.shape[1:], jnp.float32)

    @pl.when(jnp.logical_not(has_low))
    def _():
        prov[0, 0] = jnp.zeros(prov.shape[2:], jnp.float32)
        p1[0:2] = jnp.zeros((2,) + p1.shape[1:], jnp.float32)
        part_in[0] = jnp.zeros(part_in.shape[1:], jnp.float32)

    pl.semaphore_wait(barrier, n - 1)

    @pl.when(has_low)
    def _():
        feed(me).start()
        halo(False).start()

    @pl.when(has_high)
    def _():
        halo(True).start()

    zeros = jnp.zeros((16, rows.shape[1]), jnp.float32)
    rows[...] = zeros
    owners = 256 // SLOT
    wide = owners * cap
    source_lane = lax.broadcasted_iota(jnp.int32, (wide, 256), 0)
    slot_lane = lax.broadcasted_iota(jnp.int32, (wide, 256), 1)
    within = slot_lane & (SLOT - 1)
    picked = (source_lane == (slot_lane >> 4) * cap + within) & (within < cap)
    pick = jnp.where(picked, 1.0, 0.0)
    chunks = n // owners
    for copy in small:
        copy.wait()
    rows[0:3] = motion_in[...]
    rows[3:6] = axis_in[...]
    rows[6:7] = chord_in[...]
    rows[8:9] = (cell_in[...] + 1).astype(jnp.float32)
    rows[9:12] = frac_in[...]
    for q in range(chunks):
        spaced = lax.dot_general(
            rows[:, q * wide : (q + 1) * wide],
            pick,
            (((1,), (0,)), ((), ())),
            precision=lax.Precision.HIGHEST,
            preferred_element_type=jnp.float32,
        )
        table[q] = spaced[8:16]
        for h in range(256 // LANES):
            blocks[q * (256 // LANES) + h] = spaced[0:8, h * LANES : (h + 1) * LANES]

    per = LANES // SLOT

    def blade(k, to, slot):
        return pltpu.make_async_remote_copy(
            src_ref=blocks.at[to // per],
            dst_ref=arrived.at[slot],
            send_sem=blade_send.at[k],
            recv_sem=blade_recv.at[k],
            device_id={"gx": to},
            device_id_type=MESH,
        )

    def send_blade(k, carry):
        blade(k, lax.rem(me + k, n), me).start()
        return carry

    lax.fori_loop(1, n, send_blade, 0)
    arrived[me] = blocks[me // per]

    def wrap(ref, *lead):
        ref[(*lead, slice(PAD - 1, PAD))] = ref[(*lead, slice(PAD + ny - 1, PAD + ny))]
        ref[(*lead, slice(PAD + ny, PAD + ny + 1))] = ref[(*lead, slice(PAD, PAD + 1))]

    load.wait()
    for i in range(3):
        for x in range(cx):
            wrap(u, i, x + 1)

    depth_bits, span_bits = nz.bit_length() - 1, ny.bit_length() - 1
    layer = lax.broadcasted_iota(jnp.int32, (LANES, 256), 0)

    def weights(q):
        info = table[q]
        where = (info[0:1] + 0.5).astype(jnp.int32) - 1
        full = where >= 0
        a = where >> (depth_bits + span_bits)
        b = (where >> depth_bits) & (ny - 1)
        d = where & (nz - 1)
        fx, fy, fz = info[1:2], info[2:3], info[3:4]
        along_z = jnp.where(layer == d, 1.0 - fz, jnp.where(layer == d + 1, fz, 0.0))
        next_b = (b + 1) & (ny - 1)
        along_y = jnp.where(layer == b, 1.0 - fy, jnp.where(layer == next_b, fy, 0.0))
        along_x = []
        for x in range(cx):
            kept = jnp.where(a == x, 1.0 - fx, jnp.where(a + 1 == x, fx, 0.0))
            along_x.append(jnp.where(full, kept, 0.0))
        return along_x, along_y, split(along_z)

    sampled = []
    for q in range(chunks):
        along_x, along_y, along_z = weights(q)
        for i in range(3):
            total = jnp.zeros((1, 256), jnp.float32)
            for x in range(cx):
                lines = product(split(u[i, x + 1, body]), along_z, ((1,), (0,)))
                total = total + along_x[x] * jnp.sum(lines * along_y, axis=0, keepdims=True)
            sampled.append(total)

    first = lax.broadcasted_iota(jnp.int32, (ROWS, nz), 1) == 0
    last = lax.broadcasted_iota(jnp.int32, (ROWS, nz), 1) == nz - 1

    def deeper(value, edge=0.0):
        return jnp.where(last, edge, pltpu.roll(value, nz - 1, 1))

    def shallower(value, edge=0.0):
        return jnp.where(first, edge, pltpu.roll(value, 1, 1))

    starts = range(PAD, PAD + ny, ROWS)

    def at(start, shift=0):
        return pl.ds(start + shift, ROWS)

    def viscosity(p, low, mid, up):
        for s in starts:
            d = []
            for i in range(3):
                centre = u[i, mid, at(s)]
                d.append(
                    (
                        u[i, up, at(s)] - u[i, low, at(s)],
                        u[i, mid, at(s, 1)] - u[i, mid, at(s, -1)],
                        deeper(centre) - shallower(centre),
                    )
                )
            xy, xz, yz = d[0][1] + d[1][0], d[0][2] + d[2][0], d[1][2] + d[2][1]
            shear = d[0][0] * d[0][0] + d[1][1] * d[1][1] + d[2][2] * d[2][2]
            shear = shear + shear + (xy * xy + xz * xz + yz * yz) + 4.0 * STRAIN_FLOOR
            nu[p, at(s)] = (0.25 * TIME_STEP * SMAGORINSKY) * jnp.sqrt(shear)
        wrap(nu, p)

    def inner_viscosity(p, carry):
        viscosity(p + 1, p, p + 1, p + 2)
        return carry

    lax.fori_loop(1, cx - 1, inner_viscosity, 0)

    @pl.when(has_low)
    def _():
        halo(True).wait_recv()

    @pl.when(jnp.logical_not(has_low))
    def _():
        def take_inlet(k, carry):
            feed(k).wait_recv()
            return carry

        lax.fori_loop(1, n, take_inlet, 0)
        own = pltpu.make_async_copy(inflow, inlet.at[0], own_sem)
        own.start()
        own.wait()
        share = inflow.shape[1]
        for k in range(n):
            at = slice(PAD + k * share, PAD + (k + 1) * share)
            for i in range(3):
                u[i, 0, at] = inlet[k, i]

    for i in range(3):
        wrap(u, i, 0)

    def layer_of(up):
        return pltpu.make_async_remote_copy(
            src_ref=nu.at[cx if up else 1, body],
            dst_ref=nu.at[0 if up else cx + 1, body],
            send_sem=nu_send.at[int(up)],
            recv_sem=nu_recv.at[int(up)],
            device_id={"gx": me + 1 if up else me - 1},
            device_id_type=MESH,
        )

    viscosity(1, 0, 1, 2)

    @pl.when(has_low)
    def _():
        layer_of(False).start()

    @pl.when(has_high)
    def _():
        halo(False).wait_recv()

    for i in range(3):
        wrap(u, i, cx + 1)
    viscosity(cx, cx - 1, cx, cx + 1)

    @pl.when(has_high)
    def _():
        layer_of(True).start()

    @pl.when(jnp.logical_not(has_low))
    def _():
        viscosity(0, 0, 0, 1)

    @pl.when(jnp.logical_not(has_high))
    def _():
        viscosity(cx + 1, cx, cx + 1, cx + 1)

    def take_blade(k, carry):
        blade(k, me, lax.rem(me + n - k, n)).wait_recv()
        return carry

    lax.fori_loop(1, n, take_blade, 0)
    lane = lax.broadcasted_iota(jnp.int32, (8, LANES), 1)
    mine = lax.rem(me, per)
    for q in range(chunks):
        halves = []
        for h in range(256 // LANES):
            block = jnp.zeros((8, LANES), jnp.float32)
            for o in range(per):
                shift = lax.rem(o - mine + per, per) * SLOT
                moved = pltpu.roll(arrived[(q * (256 // LANES) + h) * per + o], shift, 1)
                block = jnp.where((lane >> 4) == o, moved, block)
            halves.append(block)
        point = jnp.concatenate(halves, axis=1)
        along_x, along_y, along_z = weights(q)
        r = [sampled[3 * q + i] - point[i : i + 1] for i in range(3)]
        e = [point[3 + i : 4 + i] for i in range(3)]
        speed = jnp.sqrt(r[0] * r[0] + r[1] * r[1] + r[2] * r[2] + STRAIN_FLOOR)
        size = (TIME_STEP * FORCE_SCALE) * point[6:7] * speed
        lift = [
            r[1] * e[2] - r[2] * e[1],
            r[2] * e[0] - r[0] * e[2],
            r[0] * e[1] - r[1] * e[0],
        ]
        for i in range(3):
            force = size * (lift[i] - r[i])
            for x in range(cx):
                laid = product(
                    split(along_y * (force * along_x[x])), along_z, ((1,), (1,))
                )
                if q == 0:
                    prov[i, x + 1, body] = laid
                else:
                    prov[i, x + 1, body] += laid

    def momentum(p):
        for s in starts:
            centre = [u[i, p + 1, at(s)] for i in range(3)]
            own = nu[p + 1, at(s)]
            edge = centre[2] * centre[2]
            edge = edge + edge + centre[0] * centre[0] + centre[1] * centre[1]
            edge = (0.25 * TIME_STEP * SMAGORINSKY) * jnp.sqrt(edge + 4.0 * STRAIN_FLOOR)
            carried = [(0.5 * TIME_STEP) * value for value in centre]
            coef = [
                own + nu[p + 2, at(s)] - carried[0],
                own + nu[p, at(s)] + carried[0],
                own + nu[p + 1, at(s, 1)] - carried[1],
                own + nu[p + 1, at(s, -1)] + carried[1],
                own + deeper(own, edge) - carried[2],
                own + shallower(own, edge) + carried[2],
            ]
            rest = 1.0 - (coef[0] + coef[1] + coef[2] + coef[3] + coef[4] + coef[5])
            for i in range(3):
                value = prov[i, p + 1, at(s)] + rest * centre[i]
                value = value + coef[0] * u[i, p + 2, at(s)] + coef[1] * u[i, p, at(s)]
                value = value + coef[2] * u[i, p + 1, at(s, 1)] + coef[3] * u[i, p + 1, at(s, -1)]
                value = value + coef[4] * deeper(centre[i]) + coef[5] * shallower(centre[i])
                prov[i, p + 1, at(s)] = value
        wrap(prov, 1, p + 1)

    def inner_momentum(p, carry):
        momentum(p)
        return carry

    lax.fori_loop(1, cx - 1, inner_momentum, 0)

    scale = -1.0 / 12.0

    def flat_part(p, s):
        w = prov[2, p + 1, at(s)]
        return prov[1, p + 1, at(s, 1)] - prov[1, p + 1, at(s, -1)] + deeper(w) - shallower(w)

    def rim(up, what):
        if what == 0:
            src = prov.at[0, cx if up else 1, body]
            dst = prov.at[0, 0 if up else cx + 1, body]
        elif what == 1:
            src = part_out.at[1 if up else 0]
            dst = part_in.at[0 if up else 1]
        else:
            plane = cx - 5 + what if up else what - 1
            src = p1.at[plane + 3, body]
            dst = p1.at[plane + 3 - cx if up else plane + 3 + cx, body]
        k = 4 * int(up) + what
        return pltpu.make_async_remote_copy(
            src_ref=src,
            dst_ref=dst,
            send_sem=rim_send.at[k],
            recv_sem=rim_recv.at[k],
            device_id={"gx": me + 1 if up else me - 1},
            device_id_type=MESH,
        )

    def send_rim(up, what):
        @pl.when(has_high if up else has_low)
        def _():
            rim(up, what).start()

    def first_potential(p):
        for s in starts:
            p1[p + 3, at(s)] = scale * (
                flat_part(p, s) + prov[0, p + 2, at(s)] - prov[0, p, at(s)]
            )

    @pl.when(has_low)
    def _():
        layer_of(True).wait_recv()

    momentum(0)
    send_rim(False, 0)
    for s in starts:
        part_out[0, pl.ds(s - PAD, ROWS)] = scale * (flat_part(0, s) + prov[0, 2, at(s)])
    send_rim(False, 1)
    for p in range(1, cx - 2):
        first_potential(p)
    send_rim(False, 2)
    send_rim(True, 2)

    @pl.when(has_high)
    def _():
        layer_of(False).wait_recv()

    momentum(cx - 1)
    send_rim(True, 0)
    for s in starts:
        part_out[1, pl.ds(s - PAD, ROWS)] = scale * (
            flat_part(cx - 1, s) - prov[0, cx - 1, at(s)]
        )
    send_rim(True, 1)
    first_potential(cx - 2)
    send_rim(False, 3)
    send_rim(True, 3)
    for p in range(1, cx - 1):
        wrap(p1, p + 3)

    for what in range(4):

        @pl.when(has_low)
        def _():
            rim(True, what).wait_recv()

        @pl.when(has_high)
        def _():
            rim(False, what).wait_recv()

    for s in starts:
        o = pl.ds(s - PAD, ROWS)
        p1[3, at(s)] = part_out[0, o] - scale * prov[0, 0, at(s)]
        p1[cx + 2, at(s)] = part_out[1, o] + scale * prov[0, cx + 1, at(s)]
        p1[2, at(s)] = low_ok * (part_in[0, o] + scale * prov[0, 1, at(s)])
        p1[cx + 3, at(s)] = high_ok * (part_in[1, o] - scale * prov[0, cx, at(s)])
    for p in (1, 2, 3, cx + 2, cx + 3, cx + 4):
        wrap(p1, p)

    def sweep(old, new, back):
        planes = new.shape[0]
        outer = (planes - cx) // 2

        def plane(p, carry):
            ok = jnp.where(p < outer, low_ok, jnp.where(p >= outer + cx, high_ok, 1.0))
            for s in starts:
                centre = old[p + 1, at(s)]
                near = old[p, at(s)] + old[p + 2, at(s)]
                near = near + old[p + 1, at(s, 1)] + old[p + 1, at(s, -1)]
                near = near + deeper(centre) + shallower(centre)
                new[p, at(s)] = ok * (near * (1.0 / 6.0) + p1[p + back, at(s)])
            wrap(new, p)
            return carry

        lax.fori_loop(0, planes, plane, 0)

    sweep(p1, p2, 1)
    sweep(p2, p3, 2)

    def store(p):
        return pltpu.make_async_copy(result.at[:, p], change.at[:, p], store_sem.at[p])

    def correct(p, carry):
        for s in starts:
            o = pl.ds(s - PAD, ROWS)
            centre = p3[p + 1, at(s)]
            result[0, p, o] = prov[0, p + 1, at(s)] - 0.5 * (p3[p + 2, at(s)] - p3[p, at(s)])
            result[1, p, o] = prov[1, p + 1, at(s)] - 0.5 * (p3[p + 1, at(s, 1)] - p3[p + 1, at(s, -1)])
            result[2, p, o] = prov[2, p + 1, at(s)] - 0.5 * (deeper(centre) - shallower(centre))
        store(p).start()
        return carry

    lax.fori_loop(0, cx, correct, 0)

    def sent_blade(k, carry):
        blade(k, lax.rem(me + k, n), me).wait_send()
        return carry

    lax.fori_loop(1, n, sent_blade, 0)
    for p in range(cx):
        store(p).wait()

    @pl.when(has_low)
    def _():
        feed(me).wait_send()
        halo(False).wait_send()
        layer_of(False).wait_send()
        for what in range(4):
            rim(False, what).wait_send()

    @pl.when(has_high)
    def _():
        halo(True).wait_send()
        layer_of(True).wait_send()
        for what in range(4):
            rim(True, what).wait_send()


def shards(n, velocity, inflow, blade_motion, blade_axis, blade_chord, host_cell, host_frac):
    cx, ny, nz = velocity.shape[1:]
    slots = host_cell.shape[0]
    high = PAD + ny + 8
    vmem = pltpu.VMEM
    f32 = jnp.float32
    dma = pltpu.SemaphoreType.DMA
    return pl.pallas_call(
        functools.partial(kernel, n),
        out_shape=jax.ShapeDtypeStruct(velocity.shape, f32),
        in_specs=[pl.BlockSpec(memory_space=pltpu.HBM)] * 7,
        out_specs=pl.BlockSpec(memory_space=pltpu.HBM),
        scratch_shapes=[
            vmem((3, slots), f32),
            vmem((3, slots), f32),
            vmem((1, slots), f32),
            vmem((1, slots), jnp.int32),
            vmem((3, slots), f32),
            vmem((3, cx + 2, high, nz), f32),
            vmem((cx + 2, high, nz), f32),
            vmem((3, cx + 2, high, nz), f32),
            vmem((cx + 6, high, nz), f32),
            vmem((cx + 4, high, nz), f32),
            vmem((cx + 2, high, nz), f32),
            vmem((2, ny, nz), f32),
            vmem((2, ny, nz), f32),
            vmem((16, slots), f32),
            vmem((n * SLOT // LANES, 8, LANES), f32),
            vmem((n * SLOT // 256, 8, 256), f32),
            vmem((n, 8, LANES), f32),
            vmem((n,) + inflow.shape, f32),
            dma,
            dma((5,)),
            dma,
            dma((2,)),
            dma((2,)),
            dma((n,)),
            dma((n,)),
            dma,
            dma((n,)),
            dma((2,)),
            dma((2,)),
            dma((8,)),
            dma((8,)),
            vmem(velocity.shape, f32),
            dma((cx,)),
        ],
        compiler_params=pltpu.CompilerParams(
            collective_id=0, has_side_effects=True, vmem_limit_bytes=64 * 1024 * 1024 - 65536
        ),
    )(
        velocity,
        inflow,
        blade_motion,
        blade_axis,
        blade_chord.reshape(1, slots),
        host_cell.reshape(1, slots),
        host_frac,
    )


def solution(mesh):
    return jax.shard_map(
        functools.partial(shards, mesh.shape["gx"]),
        mesh=mesh,
        in_specs=(
            P("runs", "gx", None, None),
            P("runs", "gx", None),
            P("runs", "gx"),
            P("runs", "gx"),
            P(("runs", "gx")),
            P(("runs", "gx")),
            P("runs", "gx"),
        ),
        out_specs=P("runs", "gx", None, None),
        check_vma=False,
    )
```
